32 devices in a mesh: dp: 8 (over y, x, core), replica: 4 (over z).
Axes of the slice: x: 2, y: 2, z: 4, core: 2. Of those that a mesh axis runs over, the one named last changes fastest.
Arguments:
- tokens: bfloat16 [4, 1024, 1024], P('replica', 'dp'), may hold values from -6 to 6
- user_of_row: int32 [4, 1024], P('replica'), may hold values from 0 to 31, as said below
- proj_weight: bfloat16 [1024, 1536], replicated
- norm_gain: float32 [512], replicated, may hold values from 0.5 to 1.5
- grad_out: bfloat16 [4, 2048, 512], P('replica', 'dp'), may hold values from -6 to 6
Outputs:
- attended: bfloat16 [4, 2048, 512], P('replica', 'dp')
- grad_tokens: bfloat16 [4, 1024, 1024], P('replica', 'dp')
- grad_weight: float32 [1024, 1536], P('dp')
The draws below stay inside these ranges and needn't reach their ends.
Inputs may be any that keep to these rules, and one draw needn't show every extreme that they name: `user_of_row`: user u belongs to owner u // 4. Among the 128 rows of one source device in one batch at most 32 belong to users of any one owner, and in every batch one owner gets exactly 32 rows from every source.
All inputs are finite; a program needn't handle non-finite values.
Results may differ from the reference program's by a relative error of at most 0.0068.
Values may be sent and summed in bfloat16 or wider, within the bound.
No kernel may reach another device: no remote copies, remote signals or barrier semaphores. Data moves between devices by JAX's collectives and lax.ppermute only.
A program may use at most 64 MiB of HBM per device.

```python
import math
import jax
import jax.numpy as jnp
from jax import lax

D = 1024
HEADS = 4
HEAD_DIM = 128
UPO = 4
TOK_DEV = 128
HW = 512
QKV = 1536
SOURCES = 8
REPLICAS = 4
CAP = 32
SLOTS = 256
ROWS = 1024
PACKED = 2048


def draw_user_of_row(key, part):
    subkeys = jax.random.split(key, 3)
    hot_owner = jax.random.randint(subkeys[0], (REPLICAS, 1, 1), 0, SOURCES)
    source_keys = jax.random.split(subkeys[1], REPLICAS * SOURCES)

    def one_source(source_key):
        first_key, second_key = jax.random.split(source_key)
        others = CAP + jax.random.permutation(first_key, SOURCES * CAP - CAP)[:TOK_DEV - CAP]
        chosen = jnp.concatenate([jnp.arange(CAP, dtype=jnp.int32), others.astype(jnp.int32)])
        return jax.random.permutation(second_key, chosen)
    chosen_all = jax.vmap(one_source)(source_keys).reshape(REPLICAS, SOURCES, TOK_DEV)
    owners = (chosen_all // CAP + hot_owner) % SOURCES
    within = jax.random.randint(subkeys[2], (REPLICAS, SOURCES, TOK_DEV), 0, UPO)
    return (owners * UPO + within).reshape(REPLICAS, ROWS).astype(jnp.int32)


def draw_proj_weight(key, part):
    entry_key, scale_key = jax.random.split(key)
    entries = jax.random.normal(entry_key, (D, QKV), jnp.float32)
    scales = jnp.exp(jax.random.uniform(scale_key, (1, QKV), jnp.float32, math.log(0.35), math.log(3.5)))
    return (entries * scales / math.sqrt(D)).astype(jnp.bfloat16)


def strengthened(array, rng, source, target, parts, factor):
    def block_of(dim):
        return (jnp.arange(array.shape[dim]) // (array.shape[dim] // parts)).reshape((-1,) + (1,) * (array.ndim - 1 - dim))

    first = jax.random.permutation(rng, parts)[block_of(target)]
    other_side = (block_of(target) + parts // 2) % parts
    return jnp.where((block_of(source) == first) | (block_of(source) == other_side), factor * array, array)


def level_of(key, extent, pieces, least, top_value):
    loudness = 1.0
    for axis_at, parts in pieces:
        draws = jax.random.uniform(jax.random.fold_in(jax.random.fold_in(key, 6), axis_at), (parts,), jnp.float32, least / len(pieces), top_value / len(pieces))
        loudness = loudness * jnp.repeat(jnp.exp(draws), extent[axis_at] // parts).reshape((-1,) + (1,) * (len(extent) - 1 - axis_at))
    return loudness


def normal_values(rng, shape, deviation, bound, cuts=(), held_as=jnp.bfloat16):
    result = deviation * jax.random.normal(rng, shape, jnp.float32)
    if cuts:
        result = result * level_of(rng, shape, cuts, -0.22, 0.18)
    return jnp.clip(result, -bound, bound).astype(held_as)


def noise_with(rng, dims, width, limit, pieces, heavy, kind=jnp.bfloat16):
    array = width * jax.random.normal(rng, dims, jnp.float32)
    if pieces:
        array = array * level_of(rng, dims, pieces, -0.22, 0.18)
    return jnp.clip(strengthened(array, jax.random.fold_in(rng, 3), *heavy), -limit, limit).astype(kind)


def setup_inputs(seed: int = 0) -> dict:
    seeds = jax.random.split(jax.random.key(seed), 6)
    tokens = noise_with(seeds[0], (REPLICAS, ROWS, D), 1.0, 6.0, ((0, 4), (1, 8)), (1, 2, 8, 2.0))
    user_of_row = draw_user_of_row(jax.random.fold_in(seeds[5], 71), 0)
    proj_weight = draw_proj_weight(jax.random.fold_in(seeds[5], 71), 0)
    norm_gain = jnp.clip(1.0 + 0.1 * jax.random.normal(seeds[3], (HW,), jnp.float32), 0.5, 1.5)
    grad_out = normal_values(seeds[4], (REPLICAS, PACKED, HW), 1.0, 6.0, ((0, 4), (1, 8)))
    return {"tokens": tokens, "user_of_row": user_of_row, "proj_weight": proj_weight, "norm_gain": norm_gain, "grad_out": grad_out}


def silu_grad(preact):
    sigmoid_p = jax.nn.sigmoid(preact)
    return sigmoid_p * (1.0 + preact * (1.0 - sigmoid_p))

def attend(activated, gain, slot_user, slot_order):
    slot_total = activated.shape[0]
    split_acts = activated.astype(jnp.float32).reshape(slot_total, 3, HEADS, HEAD_DIM)
    queries = split_acts[:, 0]
    keys_h = split_acts[:, 1]
    values = split_acts[:, 2]
    scores = jnp.einsum('qhd,khd->hqk', queries, keys_h, precision=lax.Precision.HIGHEST) * HEAD_DIM ** (-0.5)
    visible = (slot_user[:, None] == slot_user[None, :]) & (slot_order[None, :] <= slot_order[:, None]) & (slot_user[:, None] >= 0)
    weights = jnp.where(visible[None], jax.nn.silu(scores), 0.0)
    mixed = jnp.einsum('hqk,khd->qhd', weights, values, precision=lax.Precision.HIGHEST).reshape(slot_total, HEADS * HEAD_DIM)
    mean_row = lax.optimization_barrier(jnp.mean(mixed, axis=1, keepdims=True))
    centered = mixed - mean_row
    variance = lax.optimization_barrier(jnp.mean(centered * centered, axis=1, keepdims=True))
    return centered * lax.rsqrt(variance + 1e-06) * gain

def block_pass(activated, gain, slot_user, slot_order, cotangent):

    def forward(acts):
        return attend(acts, gain, slot_user, slot_order)
    normed, pull = jax.vjp(forward, activated)
    d_acts, = pull(cotangent.astype(jnp.float32))
    return (normed.astype(jnp.bfloat16), d_acts)

def reference(tokens, user_of_row, proj_weight, norm_gain, grad_out):
    user_ids = user_of_row.reshape(REPLICAS, SOURCES, TOK_DEV)
    owners = user_ids // UPO
    matches = (owners[..., None] == jnp.arange(SOURCES, dtype=jnp.int32)[None, None, None, :]).astype(jnp.int32)
    in_rank = lax.optimization_barrier(jnp.sum(jnp.cumsum(matches, axis=2) * matches, axis=3)) - 1
    sources_iota = jnp.arange(SOURCES, dtype=jnp.int32)[None, :, None]
    target = (owners * SLOTS + sources_iota * CAP + in_rank).reshape(REPLICAS, ROWS).astype(jnp.int32)
    rows_flat = tokens.reshape(REPLICAS * ROWS, D)
    preact = jnp.dot(rows_flat, proj_weight, preferred_element_type=jnp.float32)
    activated = jax.nn.silu(preact).astype(jnp.bfloat16).reshape(REPLICAS, ROWS, QKV)
    replica_iota = jnp.arange(REPLICAS, dtype=jnp.int32)[:, None]
    packed = jnp.zeros((REPLICAS, PACKED, QKV), activated.dtype).at[replica_iota, target].set(activated)
    slot_user = jnp.full((REPLICAS, PACKED), -1, jnp.int32).at[replica_iota, target].set(user_of_row.astype(jnp.int32))
    order_rows = jnp.broadcast_to(jnp.arange(ROWS, dtype=jnp.int32)[None, :], (REPLICAS, ROWS))
    slot_order = jnp.zeros((REPLICAS, PACKED), jnp.int32).at[replica_iota, target].set(order_rows)

    def one_block(inputs):
        return block_pass(inputs[0], norm_gain, inputs[1], inputs[2], inputs[3])
    attended, d_packed = lax.map(one_block, (packed.reshape(REPLICAS * SOURCES, SLOTS, QKV), slot_user.reshape(REPLICAS * SOURCES, SLOTS), slot_order.reshape(REPLICAS * SOURCES, SLOTS), grad_out.reshape(REPLICAS * SOURCES, SLOTS, HW)))
    d_rows = d_packed.reshape(REPLICAS, PACKED, QKV)[replica_iota, target].reshape(REPLICAS * ROWS, QKV)
    d_rows = lax.optimization_barrier(d_rows)
    d_pre = (d_rows.astype(jnp.float32) * silu_grad(preact)).astype(jnp.bfloat16)
    grad_tokens = jnp.dot(d_pre, proj_weight.T, preferred_element_type=jnp.float32).astype(jnp.bfloat16).reshape(REPLICAS, ROWS, D)
    grad_weight = jnp.dot(rows_flat.T, d_pre, preferred_element_type=jnp.float32)
    return (attended.reshape(REPLICAS, PACKED, HW), grad_tokens, grad_weight)
```

```python
import functools

import jax
import jax.numpy as jnp
from jax import lax
from jax.experimental import pallas as pl
from jax.experimental.pallas import tpu as pltpu
from jax.sharding import PartitionSpec as P

HEADS = 4
HEAD_DIM = 128
UPO = 4


def silu_grad(preact):
    sigmoid_p = jax.nn.sigmoid(preact)
    return sigmoid_p * (1.0 + preact * (1.0 - sigmoid_p))


def attend(activated, gain, slot_user, slot_order):
    slot_total = activated.shape[0]
    split_acts = activated.astype(jnp.float32).reshape(slot_total, 3, HEADS, HEAD_DIM)
    queries = split_acts[:, 0]
    keys_h = split_acts[:, 1]
    values = split_acts[:, 2]
    scores = jnp.einsum(
        "qhd,khd->hqk", queries, keys_h, precision=lax.Precision.HIGHEST
    ) * HEAD_DIM ** (-0.5)
    visible = (
        (slot_user[:, None] == slot_user[None, :])
        & (slot_order[None, :] <= slot_order[:, None])
        & (slot_user[:, None] >= 0)
    )
    weights = jnp.where(visible[None], jax.nn.silu(scores), 0.0)
    mixed = jnp.einsum("hqk,khd->qhd", weights, values, precision=lax.Precision.HIGHEST).reshape(
        slot_total, HEADS * HEAD_DIM
    )
    mean_row = jnp.mean(mixed, axis=1, keepdims=True)
    centered = mixed - mean_row
    variance = jnp.mean(centered * centered, axis=1, keepdims=True)
    return centered * lax.rsqrt(variance + 1e-06) * gain


def block_pass(activated, gain, slot_user, slot_order, cotangent):

    def forward(acts):
        return attend(acts, gain, slot_user, slot_order)

    normed, pull = jax.vjp(forward, activated)
    (d_acts,) = pull(cotangent.astype(jnp.float32))
    return (normed.astype(jnp.bfloat16), d_acts)


def general_body(tokens, user_of_row, proj_weight, norm_gain, grad_out):
    peer_count = lax.axis_size("dp")
    self_index = lax.axis_index("dp")
    row_count = tokens.shape[1]
    width = proj_weight.shape[0]
    capacity = 2 * row_count // peer_count
    slot_count = peer_count * capacity
    routing = user_of_row[0]
    owners = (routing // UPO).reshape(peer_count, row_count)
    peer_ids = jnp.arange(peer_count, dtype=jnp.int32)
    inbound = (owners == self_index).astype(jnp.int32)
    in_rank = jnp.cumsum(inbound, axis=1) - 1
    matches = (
        (inbound[:, None, :] == 1)
        & (in_rank[:, None, :] == jnp.arange(capacity, dtype=jnp.int32)[None, :, None])
    ).astype(jnp.int32)
    users_src = routing.reshape(peer_count, row_count)
    slot_user = jnp.sum(matches * (users_src[:, None, :] + 1), axis=2).reshape(slot_count) - 1
    order_src = jnp.arange(peer_count * row_count, dtype=jnp.int32).reshape(peer_count, row_count)
    slot_order = jnp.sum(matches * order_src[:, None, :], axis=2).reshape(slot_count)
    own_owner = lax.dynamic_slice_in_dim(owners, self_index, 1, 0)[0]
    to_peer = (own_owner[:, None] == peer_ids[None, :]).astype(jnp.int32)
    out_rank = jnp.sum(jnp.cumsum(to_peer, axis=0) * to_peer, axis=1) - 1
    position = own_owner * capacity + out_rank
    rows_x = tokens[0]
    cotangent = grad_out[0]
    contract_cols = (((1,), (1,)), ((), ()))
    contract_rows = (((0,), (0,)), ((), ()))
    outgoing = jnp.zeros((slot_count, width), rows_x.dtype).at[position].set(rows_x)
    arrived = lax.all_to_all(outgoing, "dp", split_axis=0, concat_axis=0, tiled=True)
    preact = jnp.dot(arrived, proj_weight, preferred_element_type=jnp.float32)
    activated = jax.nn.silu(preact).astype(jnp.bfloat16)
    attended, d_acts = block_pass(activated, norm_gain, slot_user, slot_order, cotangent)
    d_acts = lax.optimization_barrier(d_acts)
    d_pre = (d_acts.astype(jnp.float32) * silu_grad(preact)).astype(jnp.bfloat16)
    d_slots = lax.dot_general(
        d_pre, proj_weight, contract_cols, preferred_element_type=jnp.float32
    ).astype(jnp.bfloat16)
    returned = lax.all_to_all(d_slots, "dp", split_axis=0, concat_axis=0, tiled=True)
    grad_tokens = returned[position]
    weight_shard = lax.psum_scatter(
        lax.dot_general(arrived, d_pre, contract_rows, preferred_element_type=jnp.float32),
        "dp",
        scatter_dimension=0,
        tiled=True,
    )
    grad_weight = lax.psum(weight_shard, "replica")
    return (attended[None], grad_tokens[None], grad_weight)


F32 = jnp.float32
BF16 = jnp.bfloat16
ROWS_BY_COLS = (((1,), (0,)), ((), ()))
COLS_BY_COLS = (((1,), (1,)), ((), ()))
ROWS_BY_ROWS = (((0,), (0,)), ((), ()))
VMEM_LIMIT = 40 * 1024 * 1024


def matmul(left, right, contract=ROWS_BY_COLS):
    return lax.dot_general(left, right, contract, preferred_element_type=F32)


def call(kernel, outs, operands, flops, scratch=()):
    nbytes = sum(a.size * a.dtype.itemsize for a in operands)
    nbytes += sum(o.size * o.dtype.itemsize for o in outs)
    vmem = pl.BlockSpec(memory_space=pltpu.VMEM)
    return pl.pallas_call(
        kernel,
        out_shape=outs,
        in_specs=[vmem] * len(operands),
        out_specs=[vmem] * len(outs),
        scratch_shapes=list(scratch),
        compiler_params=pltpu.CompilerParams(vmem_limit_bytes=VMEM_LIMIT),
        cost_estimate=pl.CostEstimate(flops=flops, bytes_accessed=nbytes, transcendentals=0),
    )(*operands)


def shaped(shape, dtype):
    return jax.ShapeDtypeStruct(shape, dtype)


def running_count(flags):
    length = flags.shape[1]
    at = lax.broadcasted_iota(jnp.int32, (length, length), 0)
    upto = lax.broadcasted_iota(jnp.int32, (length, length), 1)
    return matmul(flags, (at <= upto).astype(F32))


def own_placement(users_ref, me, peers, capacity):
    owner = lax.div(users_ref[pl.ds(me, 1), :], UPO)
    rows = owner.shape[1]
    match = (lax.broadcasted_iota(jnp.int32, (peers, rows), 0) == owner).astype(F32)
    rank = jnp.sum(running_count(match) * match, axis=0, keepdims=True) - 1.0
    key = (owner ^ me) * capacity + rank.astype(jnp.int32)
    return (lax.broadcasted_iota(jnp.int32, (peers * capacity, rows), 0) == key).astype(BF16)


def pack_kernel(peers, capacity, users_ref, tokens_ref, *out_refs):
    me = lax.axis_index("dp")
    place = own_placement(users_ref, me, peers, capacity)
    packed = matmul(place, tokens_ref[...]).astype(BF16)
    for m in range(peers):
        out_refs[m][...] = packed[m * capacity : (m + 1) * capacity]


def unpack_kernel(peers, capacity, users_ref, *refs):
    *in_refs, out_ref, held = refs
    me = lax.axis_index("dp")
    place = own_placement(users_ref, me, peers, capacity)
    for m in range(peers):
        held[m * capacity : (m + 1) * capacity, :] = in_refs[m][...]
    out_ref[...] = matmul(place, held[...], ROWS_BY_ROWS).astype(BF16)


def slot_codes(users_ref, me, peers, capacity):
    users = jnp.concatenate([users_ref[pl.ds(me ^ m, 1), :] for m in range(peers)], axis=0)
    rows = users.shape[1]
    match = (lax.div(users, UPO) == me).astype(F32)
    rank = running_count(match) * match - 1.0
    position = lax.broadcasted_iota(jnp.int32, (1, rows), 1)
    slot = lax.broadcasted_iota(jnp.int32, (capacity, rows), 0).astype(F32)
    codes = []
    for m in range(peers):
        code = (users[m : m + 1] + 1) * (peers * rows) + (me ^ m) * rows + position
        picked = jnp.where(rank[m : m + 1] == slot, code.astype(F32), 0.0)
        codes.append(jnp.sum(picked, axis=1, keepdims=True))
    return jnp.concatenate(codes, axis=0)


def attend_kernel(peers, capacity, users_ref, gain_ref, w_ref, grad_ref, *refs):
    x_refs, refs = refs[:peers], refs[peers:]
    attended_ref, d_values_ref, d_rest_ref, x_own_ref, x_sib_ref, x, act, slope, grad = refs
    me = lax.axis_index("dp")
    slots = peers * capacity
    width, columns = w_ref.shape
    features = gain_ref.shape[1]
    block = width // peers
    for m in range(peers):
        x[m * capacity : (m + 1) * capacity, :] = x_refs[m][...]
    for i in range(peers // 2):
        own_at = pl.multiple_of((me ^ (2 * i)) * block, block)
        sib_at = pl.multiple_of((me ^ (2 * i + 1)) * block, block)
        x_own_ref[:, i * block : (i + 1) * block] = x[:, pl.ds(own_at, block)]
        x_sib_ref[:, i * block : (i + 1) * block] = x[:, pl.ds(sib_at, block)]
    gain = gain_ref[...]
    for m in range(peers):
        at = pl.multiple_of((me ^ m) * capacity, capacity)
        grad[m * capacity : (m + 1) * capacity, :] = grad_ref[pl.ds(at, capacity), :].astype(F32) * gain
    step = 2 * HEAD_DIM
    for c in range(0, columns, step):
        preact = matmul(x[...], w_ref[:, c : c + step])
        gate = 0.5 * jnp.tanh(0.5 * preact) + 0.5
        silu = preact * gate
        act[:, c : c + step] = silu.astype(BF16)
        slope[:, c : c + step] = gate + silu * (1.0 - gate)

    code = slot_codes(users_ref, me, peers, capacity)
    code_of_key = jnp.broadcast_to(code, (slots, HEAD_DIM)).T[0:1]
    batch_rows = users_ref.shape[0] * users_ref.shape[1]
    whole = code.astype(jnp.int32)
    first = (lax.div(whole, batch_rows) * batch_rows).astype(F32)
    first = jnp.where(code > 0.0, first, code + 1.0)
    visible = (code_of_key <= code) & (code_of_key >= first)

    def head(base, h):
        return act[:, base + h * HEAD_DIM : base + (h + 1) * HEAD_DIM]

    scale = HEAD_DIM**-0.5
    weights, slopes, mixed = [], [], []
    for h in range(HEADS):
        scores = matmul(head(0, h), head(features, h), COLS_BY_COLS) * scale
        gate = 0.5 * jnp.tanh(0.5 * scores) + 0.5
        silu = scores * gate
        weight = jnp.where(visible, silu, 0.0).astype(BF16)
        slopes.append(jnp.where(visible, (gate + silu * (1.0 - gate)) * scale, 0.0))
        weights.append(weight)
        mixed.append(matmul(weight, head(2 * features, h)))
    mean = sum(jnp.sum(v, axis=1, keepdims=True) for v in mixed) / features
    centered = [v - mean for v in mixed]
    variance = sum(jnp.sum(v * v, axis=1, keepdims=True) for v in centered) / features
    inverse = lax.rsqrt(variance + 1e-06)
    unit = [v * inverse for v in centered]

    def part(ref, h):
        return ref[:, h * HEAD_DIM : (h + 1) * HEAD_DIM]

    grads = [part(grad, h) for h in range(HEADS)]
    for h in range(HEADS):
        normed = (unit[h] * part(gain, h)).astype(BF16)
        for m in range(peers):
            at = pl.multiple_of((me ^ m) * capacity, capacity)
            attended_ref[pl.ds(at, capacity), h * HEAD_DIM : (h + 1) * HEAD_DIM] = normed[m * capacity : (m + 1) * capacity]
    grad_mean = sum(jnp.sum(g, axis=1, keepdims=True) for g in grads) / features
    grad_unit = sum(jnp.sum(g * u, axis=1, keepdims=True) for g, u in zip(grads, unit)) / features
    for h in range(HEADS):
        d_mixed = ((grads[h] - grad_mean - unit[h] * grad_unit) * inverse).astype(BF16)
        d_value = matmul(weights[h], d_mixed, ROWS_BY_ROWS)
        at = h * HEAD_DIM
        d_values_ref[:, at : at + HEAD_DIM] = (d_value * part(slope, 2 * HEADS + h)).astype(BF16)
        d_scores = (matmul(d_mixed, head(2 * features, h), COLS_BY_COLS) * slopes[h]).astype(BF16)
        d_query = matmul(d_scores, head(features, h))
        d_key = matmul(d_scores, head(0, h), ROWS_BY_ROWS)
        d_rest_ref[:, at : at + HEAD_DIM] = (d_query * part(slope, h)).astype(BF16)
        at += features
        d_rest_ref[:, at : at + HEAD_DIM] = (d_key * part(slope, HEADS + h)).astype(BF16)


def weight_kernel(x_own_ref, x_sib_ref, d_own_ref, d_sib_ref, *out_refs):
    block = x_own_ref.shape[1] // len(out_refs)
    for i, out_ref in enumerate(out_refs):
        at = slice(i * block, (i + 1) * block)
        total = matmul(x_own_ref[:, at], d_own_ref[...], ROWS_BY_ROWS)
        total += matmul(x_sib_ref[:, at], d_sib_ref[...], ROWS_BY_ROWS)
        out_ref[...] = total.astype(out_ref.dtype)


def token_kernel(d_values_ref, d_rest_ref, w_ref, *out_refs):
    split = d_rest_ref.shape[1]
    capacity = out_refs[0].shape[0]
    total = matmul(d_rest_ref[...], w_ref[:, :split], COLS_BY_COLS)
    total += matmul(d_values_ref[...], w_ref[:, split:], COLS_BY_COLS)
    for m, out_ref in enumerate(out_refs):
        out_ref[...] = total[m * capacity : (m + 1) * capacity].astype(BF16)


def swap(array, axis, size, bits):
    return lax.ppermute(array, axis, [(i, i ^ bits) for i in range(size)])


def direct_body(tokens, user_of_row, proj_weight, norm_gain, grad_out):
    peers = lax.axis_size("dp")
    replicas = lax.axis_size("replica")
    rows = tokens.shape[1]
    width, columns = proj_weight.shape
    features = grad_out.shape[2]
    capacity = 2 * rows // peers
    slots = peers * capacity
    block = width // peers
    users = user_of_row.reshape(peers, rows)
    gain = norm_gain.reshape(1, features)
    exchange = functools.partial(swap, axis="dp", size=peers)

    outgoing = call(
        functools.partial(pack_kernel, peers, capacity),
        [shaped((capacity, width), BF16)] * peers,
        [users, tokens[0]],
        2 * slots * rows * width,
    )
    arrived = [outgoing[0]] + [exchange(outgoing[m], bits=m) for m in range(1, peers)]
    half = width // 2
    attended, d_values, d_rest, x_own, x_sib = call(
        functools.partial(attend_kernel, peers, capacity),
        [
            shaped((slots, features), BF16),
            shaped((slots, features), BF16),
            shaped((slots, columns - features), BF16),
            shaped((slots, half), BF16),
            shaped((slots, half), BF16),
        ],
        [users, gain, proj_weight, grad_out[0], *arrived],
        2 * slots * width * columns + 14 * slots * slots * features,
        [
            pltpu.VMEM((slots, width), BF16),
            pltpu.VMEM((slots, columns), BF16),
            pltpu.VMEM((slots, columns), F32),
            pltpu.VMEM((slots, features), F32),
        ],
    )
    x_from_sib = exchange(x_sib, bits=1)
    blocks = []
    for d_own in (d_values, d_rest):
        size = d_own.shape[1]
        d_from_sib = exchange(d_own, bits=1)
        mine, *others = call(
            weight_kernel,
            [shaped((block, size), F32)] + [shaped((block, size), BF16)] * (peers // 2 - 1),
            [x_own, x_from_sib, d_own, d_from_sib],
            4 * slots * half * size,
        )
        total = mine
        for i, other in enumerate(others):
            total = total + exchange(other, bits=2 * (i + 1)).astype(F32)
        bits = 1
        while bits < replicas:
            held = total.astype(BF16)
            total = held.astype(F32) + swap(held, "replica", replicas, bits).astype(F32)
            bits *= 2
        blocks.append(total)
    grad_weight = jnp.concatenate([blocks[1], blocks[0]], axis=1)

    d_slots = call(
        token_kernel,
        [shaped((capacity, width), BF16)] * peers,
        [d_values, d_rest, proj_weight],
        2 * slots * width * columns,
    )
    returned = [d_slots[0]] + [exchange(d_slots[m], bits=m) for m in range(1, peers)]
    (grad_tokens,) = call(
        functools.partial(unpack_kernel, peers, capacity),
        [shaped((rows, width), BF16)],
        [users, *returned],
        2 * slots * rows * width,
        [pltpu.VMEM((slots, width), BF16)],
    )
    return (attended[None], grad_tokens[None], grad_weight)


def power_of_two(value):
    return value & (value - 1) == 0


def body(tokens, user_of_row, proj_weight, norm_gain, grad_out):
    peers = lax.axis_size("dp")
    replicas = lax.axis_size("replica")
    capacity = 2 * tokens.shape[1] // peers
    aligned = capacity % 16 == 0 and proj_weight.shape[0] // peers % 128 == 0
    run = direct_body if aligned and power_of_two(peers) and power_of_two(replicas) else general_body
    return run(tokens, user_of_row, proj_weight, norm_gain, grad_out)


def solution(mesh):
    return jax.shard_map(
        body,
        mesh=mesh,
        in_specs=(P("replica", "dp", None), P("replica", None), P(), P(), P("replica", "dp", None)),
        out_specs=(P("replica", "dp", None), P("replica", "dp", None), P("dp", None)),
        check_vma=False,
    )
```

```python
import functools

import jax
import jax.numpy as jnp
from jax import lax
from jax.experimental import pallas as pl
from jax.experimental.pallas import tpu as pltpu
from jax.sharding import PartitionSpec as P

HEADS = 4
HEAD_DIM = 128
UPO = 4


def silu_grad(preact):
    sigmoid_p = jax.nn.sigmoid(preact)
    return sigmoid_p * (1.0 + preact * (1.0 - sigmoid_p))


def attend(activated, gain, slot_user, slot_order):
    slot_total = activated.shape[0]
    split_acts = activated.astype(jnp.float32).reshape(slot_total, 3, HEADS, HEAD_DIM)
    queries = split_acts[:, 0]
    keys_h = split_acts[:, 1]
    values = split_acts[:, 2]
    scores = jnp.einsum(
        "qhd,khd->hqk", queries, keys_h, precision=lax.Precision.HIGHEST
    ) * HEAD_DIM ** (-0.5)
    visible = (
        (slot_user[:, None] == slot_user[None, :])
        & (slot_order[None, :] <= slot_order[:, None])
        & (slot_user[:, None] >= 0)
    )
    weights = jnp.where(visible[None], jax.nn.silu(scores), 0.0)
    mixed = jnp.einsum("hqk,khd->qhd", weights, values, precision=lax.Precision.HIGHEST).reshape(
        slot_total, HEADS * HEAD_DIM
    )
    mean_row = jnp.mean(mixed, axis=1, keepdims=True)
    centered = mixed - mean_row
    variance = jnp.mean(centered * centered, axis=1, keepdims=True)
    return centered * lax.rsqrt(variance + 1e-06) * gain


def block_pass(activated, gain, slot_user, slot_order, cotangent):

    def forward(acts):
        return attend(acts, gain, slot_user, slot_order)

    normed, pull = jax.vjp(forward, activated)
    (d_acts,) = pull(cotangent.astype(jnp.float32))
    return (normed.astype(jnp.bfloat16), d_acts)


def general_body(tokens, user_of_row, proj_weight, norm_gain, grad_out):
    peer_count = lax.axis_size("dp")
    self_index = lax.axis_index("dp")
    row_count = tokens.shape[1]
    width = proj_weight.shape[0]
    capacity = 2 * row_count // peer_count
    slot_count = peer_count * capacity
    routing = user_of_row[0]
    owners = (routing // UPO).reshape(peer_count, row_count)
    peer_ids = jnp.arange(peer_count, dtype=jnp.int32)
    inbound = (owners == self_index).astype(jnp.int32)
    in_rank = jnp.cumsum(inbound, axis=1) - 1
    matches = (
        (inbound[:, None, :] == 1)
        & (in_rank[:, None, :] == jnp.arange(capacity, dtype=jnp.int32)[None, :, None])
    ).astype(jnp.int32)
    users_src = routing.reshape(peer_count, row_count)
    slot_user = jnp.sum(matches * (users_src[:, None, :] + 1), axis=2).reshape(slot_count) - 1
    order_src = jnp.arange(peer_count * row_count, dtype=jnp.int32).reshape(peer_count, row_count)
    slot_order = jnp.sum(matches * order_src[:, None, :], axis=2).reshape(slot_count)
    own_owner = lax.dynamic_slice_in_dim(owners, self_index, 1, 0)[0]
    to_peer = (own_owner[:, None] == peer_ids[None, :]).astype(jnp.int32)
    out_rank = jnp.sum(jnp.cumsum(to_peer, axis=0) * to_peer, axis=1) - 1
    position = own_owner * capacity + out_rank
    rows_x = tokens[0]
    cotangent = grad_out[0]
    contract_cols = (((1,), (1,)), ((), ()))
    contract_rows = (((0,), (0,)), ((), ()))
    outgoing = jnp.zeros((slot_count, width), rows_x.dtype).at[position].set(rows_x)
    arrived = lax.all_to_all(outgoing, "dp", split_axis=0, concat_axis=0, tiled=True)
    preact = jnp.dot(arrived, proj_weight, preferred_element_type=jnp.float32)
    activated = jax.nn.silu(preact).astype(jnp.bfloat16)
    attended, d_acts = block_pass(activated, norm_gain, slot_user, slot_order, cotangent)
    d_acts = lax.optimization_barrier(d_acts)
    d_pre = (d_acts.astype(jnp.float32) * silu_grad(preact)).astype(jnp.bfloat16)
    d_slots = lax.dot_general(
        d_pre, proj_weight, contract_cols, preferred_element_type=jnp.float32
    ).astype(jnp.bfloat16)
    returned = lax.all_to_all(d_slots, "dp", split_axis=0, concat_axis=0, tiled=True)
    grad_tokens = returned[position]
    weight_shard = lax.psum_scatter(
        lax.dot_general(arrived, d_pre, contract_rows, preferred_element_type=jnp.float32),
        "dp",
        scatter_dimension=0,
        tiled=True,
    )
    grad_weight = lax.psum(weight_shard, "replica")
    return (attended[None], grad_tokens[None], grad_weight)


F32 = jnp.float32
BF16 = jnp.bfloat16
ROWS_BY_COLS = (((1,), (0,)), ((), ()))
COLS_BY_COLS = (((1,), (1,)), ((), ()))
ROWS_BY_ROWS = (((0,), (0,)), ((), ()))
VMEM_LIMIT = 32 * 1024 * 1024
HBM = pl.BlockSpec(memory_space=pltpu.HBM)
VMEM = pl.BlockSpec(memory_space=pltpu.VMEM)


def matmul(left, right, contract=ROWS_BY_COLS):
    return lax.dot_general(left, right, contract, preferred_element_type=F32)


def call(kernel, outs, operands, flops, scratch=(), specs=None):
    nbytes = sum(a.size * a.dtype.itemsize for a in operands)
    nbytes += sum(o.size * o.dtype.itemsize for o in outs)
    return pl.pallas_call(
        kernel,
        out_shape=outs,
        in_specs=specs or [VMEM] * len(operands),
        out_specs=[VMEM] * len(outs),
        scratch_shapes=list(scratch),
        compiler_params=pltpu.CompilerParams(vmem_limit_bytes=VMEM_LIMIT),
        cost_estimate=pl.CostEstimate(flops=flops, bytes_accessed=nbytes, transcendentals=0),
    )(*operands)


def shaped(shape, dtype):
    return jax.ShapeDtypeStruct(shape, dtype)


def running_count(flags):
    length = flags.shape[1]
    at = lax.broadcasted_iota(jnp.int32, (length, length), 0)
    upto = lax.broadcasted_iota(jnp.int32, (length, length), 1)
    return matmul(flags, (at <= upto).astype(F32))


def own_placement(users_ref, me, peers, capacity):
    owner = lax.div(users_ref[pl.ds(me, 1), :], UPO)
    rows = owner.shape[1]
    match = (lax.broadcasted_iota(jnp.int32, (peers, rows), 0) == owner).astype(F32)
    rank = jnp.sum(running_count(match) * match, axis=0, keepdims=True) - 1.0
    key = (owner ^ me) * capacity + rank.astype(jnp.int32)
    return (lax.broadcasted_iota(jnp.int32, (peers * capacity, rows), 0) == key).astype(BF16)


def fetch(pairs, sems):
    copies = [pltpu.make_async_copy(src, dst, sems.at[i]) for i, (src, dst) in enumerate(pairs)]
    for copy in copies:
        copy.start()
    return copies


def pack_kernel(peers, capacity, users_hbm, tokens_hbm, *refs):
    *out_refs, users, rows, sems = refs
    users_copy, rows_copy = fetch([(users_hbm, users), (tokens_hbm, rows)], sems)
    me = lax.axis_index("dp")
    users_copy.wait()
    place = own_placement(users, me, peers, capacity)
    rows_copy.wait()
    packed = matmul(place, rows[...]).astype(BF16)
    for i, out_ref in enumerate(out_refs):
        out_ref[...] = packed[2 * i * capacity : 2 * (i + 1) * capacity]


def slot_codes(users_ref, me, peers, capacity):
    users = jnp.concatenate([users_ref[pl.ds(me ^ m, 1), :] for m in range(peers)], axis=0)
    rows = users.shape[1]
    match = (lax.div(users, UPO) == me).astype(F32)
    rank = running_count(match) * match - 1.0
    position = lax.broadcasted_iota(jnp.int32, (1, rows), 1)
    slot = lax.broadcasted_iota(jnp.int32, (capacity, rows), 0).astype(F32)
    codes = []
    for m in range(peers):
        code = (users[m : m + 1] + 1) * (peers * rows) + (me ^ m) * rows + position
        picked = jnp.where(rank[m : m + 1] == slot, code.astype(F32), 0.0)
        codes.append(jnp.sum(picked, axis=1, keepdims=True))
    return jnp.concatenate(codes, axis=0)


def prep_kernel(peers, capacity, users_hbm, gain_ref, w_hbm, grad_hbm, w_ref, grad_ref, code_ref, key_ref, users, grad, sems):
    users_copy, grad_copy, w_copy = fetch([(users_hbm, users), (grad_hbm, grad), (w_hbm, w_ref)], sems)
    me = lax.axis_index("dp")
    users_copy.wait()
    code = jnp.broadcast_to(slot_codes(users, me, peers, capacity), code_ref.shape)
    code_ref[...] = code
    key_ref[...] = code.T[0 : key_ref.shape[0]]
    grad_copy.wait()
    for m in range(peers):
        at = pl.multiple_of((me ^ m) * capacity, capacity)
        grad_ref[m * capacity : (m + 1) * capacity, :] = grad[pl.ds(at, capacity), :].astype(F32) * gain_ref[...]
    w_copy.wait()


def attend_kernel(peers, capacity, batch_rows, gain_ref, w_ref, grad, code_ref, key_ref, *refs):
    chips = peers // 2
    near, far, refs = refs[:chips], refs[chips : 2 * chips], refs[2 * chips :]
    attended_ref, *d_refs, x_own_ref, x_sib_ref, x, x_sib, act, slope = refs
    me = lax.axis_index("dp")
    slots = peers * capacity
    width, columns = w_ref.shape
    features = gain_ref.shape[1]
    block = width // peers
    first, second = slice(0, capacity), slice(capacity, 2 * capacity)
    for i in range(chips):
        even = slice(2 * i * capacity, (2 * i + 1) * capacity)
        odd = slice((2 * i + 1) * capacity, (2 * i + 2) * capacity)
        x[even, :] = near[i][first, :]
        x[odd, :] = far[i][second, :]
        x_sib[even, :] = far[i][first, :]
        x_sib[odd, :] = near[i][second, :]
    for i in range(chips):
        at = pl.multiple_of((me ^ (2 * i)) * block, block)
        x_own_ref[:, i * block : (i + 1) * block] = x[:, pl.ds(at, block)]
        x_sib_ref[:, i * block : (i + 1) * block] = x_sib[:, pl.ds(at, block)]
    gain = gain_ref[...]
    step = 2 * HEAD_DIM
    for c in range(0, columns, step):
        preact = matmul(x[...], w_ref[:, c : c + step])
        gate = 0.5 * jnp.tanh(0.5 * preact) + 0.5
        silu = preact * gate
        act[:, c : c + step] = silu.astype(BF16)
        slope[:, c : c + step] = gate + silu * (1.0 - gate)

    code = code_ref[:, 0:1]
    code_of_key = key_ref[0:1, :]
    first = (lax.div(code.astype(jnp.int32), batch_rows) * batch_rows).astype(F32)
    first = jnp.where(code > 0.0, first, code + 1.0)
    visible = (code_of_key <= code) & (code_of_key >= first)

    def head(base, h):
        return act[:, base + h * HEAD_DIM : base + (h + 1) * HEAD_DIM]

    scale = HEAD_DIM**-0.5
    weights, slopes, mixed = [], [], []
    for h in range(HEADS):
        scores = matmul(head(0, h), head(features, h), COLS_BY_COLS) * scale
        gate = 0.5 * jnp.tanh(0.5 * scores) + 0.5
        silu = scores * gate
        weight = jnp.where(visible, silu, 0.0).astype(BF16)
        slopes.append(jnp.where(visible, (gate + silu * (1.0 - gate)) * scale, 0.0))
        weights.append(weight)
        mixed.append(matmul(weight, head(2 * features, h)))
    mean = sum(jnp.sum(v, axis=1, keepdims=True) for v in mixed) / features
    centered = [v - mean for v in mixed]
    variance = sum(jnp.sum(v * v, axis=1, keepdims=True) for v in centered) / features
    inverse = lax.rsqrt(variance + 1e-06)
    unit = [v * inverse for v in centered]

    def part(ref, h):
        return ref[:, h * HEAD_DIM : (h + 1) * HEAD_DIM]

    grads = [part(grad, h) for h in range(HEADS)]
    for h in range(HEADS):
        normed = (unit[h] * part(gain, h)).astype(BF16)
        for m in range(peers):
            at = pl.multiple_of((me ^ m) * capacity, capacity)
            attended_ref[pl.ds(at, capacity), h * HEAD_DIM : (h + 1) * HEAD_DIM] = normed[m * capacity : (m + 1) * capacity]
    grad_mean = sum(jnp.sum(g, axis=1, keepdims=True) for g in grads) / features
    grad_unit = sum(jnp.sum(g * u, axis=1, keepdims=True) for g, u in zip(grads, unit)) / features
    per = HEADS // len(d_refs)
    for h in range(HEADS):
        d_ref, at = d_refs[h // per], (h % per) * HEAD_DIM
        d_mixed = ((grads[h] - grad_mean - unit[h] * grad_unit) * inverse).astype(BF16)
        d_scores = (matmul(d_mixed, head(2 * features, h), COLS_BY_COLS) * slopes[h]).astype(BF16)
        d_query = matmul(d_scores, head(features, h))
        d_key = matmul(d_scores, head(0, h), ROWS_BY_ROWS)
        d_value = matmul(weights[h], d_mixed, ROWS_BY_ROWS)
        for j, d in enumerate((d_query, d_key, d_value)):
            to = j * per * HEAD_DIM + at
            d_ref[:, to : to + HEAD_DIM] = (d * part(slope, j * HEADS + h)).astype(BF16)


def weight_block(i, x_own_ref, x_sib_ref, d_own_ref, d_sib_ref, block):
    at = slice(i * block, (i + 1) * block)
    total = matmul(x_own_ref[:, at], d_own_ref[...], ROWS_BY_ROWS)
    return total + matmul(x_sib_ref[:, at], d_sib_ref[...], ROWS_BY_ROWS)


def weight_kernel(x_own_ref, x_sib_ref, d_own_ref, d_sib_ref, *out_refs):
    block = x_own_ref.shape[1] // len(out_refs)
    for i, out_ref in enumerate(out_refs):
        out_ref[...] = weight_block(i, x_own_ref, x_sib_ref, d_own_ref, d_sib_ref, block).astype(out_ref.dtype)


def halves(half):
    side = lax.rem(lax.axis_index("replica"), 2)
    return pl.multiple_of(side * half, half), pl.multiple_of((1 - side) * half, half)


def weight_halves_kernel(blocks, x_own_ref, x_sib_ref, d_own_ref, d_sib_ref, keep_ref, send_ref, held):
    block = held.shape[0]
    half = block // 2
    keep_at, send_at = halves(half)
    for i in range(blocks):
        held[...] = weight_block(i, x_own_ref, x_sib_ref, d_own_ref, d_sib_ref, block)
        rows = slice(i * half, (i + 1) * half)
        keep_ref[rows, :] = held[pl.ds(keep_at, half), :]
        send_ref[rows, :] = held[pl.ds(send_at, half), :].astype(BF16)


def sum_halves_kernel(own_ref, *refs):
    *in_refs, keep_ref, send_ref, held = refs
    half = held.shape[0] // 2
    total = own_ref[...]
    for in_ref in in_refs:
        total = total + in_ref[...].astype(F32)
    held[...] = total
    keep_at, send_at = halves(half)
    keep_ref[...] = held[pl.ds(keep_at, half), :]
    send_ref[...] = held[pl.ds(send_at, half), :].astype(BF16)


def sum_blocks_kernel(keep_ref, in_ref, *out_refs):
    half = out_refs[0].shape[0]
    for i, out_ref in enumerate(out_refs):
        rows = slice(i * half, (i + 1) * half)
        out_ref[...] = (keep_ref[rows, :] + in_ref[rows, :].astype(F32)).astype(out_ref.dtype)


def join_kernel(features, *refs):
    *in_refs, out_ref = refs
    half, size = in_refs[0].shape
    keep_at, send_at = halves(half)
    per = size // 3
    for p in range(len(in_refs) // 2):
        for in_ref, at in ((in_refs[2 * p], keep_at), (in_refs[2 * p + 1], send_at)):
            for j in range(3):
                to = j * features + p * per
                out_ref[pl.ds(at, half), to : to + per] = in_ref[:, j * per : (j + 1) * per].astype(F32)


def token_kernel(features, w_ref, *refs):
    d_refs, out_refs = refs[:2], refs[2:]
    rows = out_refs[0].shape[0]
    per = d_refs[0].shape[1] // 3
    total = None
    for p, d_ref in enumerate(d_refs):
        for j in range(3):
            at = j * features + p * per
            term = matmul(d_ref[:, j * per : (j + 1) * per], w_ref[:, at : at + per], COLS_BY_COLS)
            total = term if total is None else total + term
    for i, out_ref in enumerate(out_refs):
        out_ref[...] = total[i * rows : (i + 1) * rows].astype(BF16)


def unpack_kernel(peers, capacity, users_hbm, *refs):
    chips = peers // 2
    near, far, (out_ref, held, users, sems) = refs[:chips], refs[chips : 2 * chips], refs[2 * chips :]
    (users_copy,) = fetch([(users_hbm, users)], sems)
    me = lax.axis_index("dp")
    for i in range(chips):
        held[2 * i * capacity : (2 * i + 1) * capacity, :] = near[i][0:capacity, :]
        held[(2 * i + 1) * capacity : (2 * i + 2) * capacity, :] = far[i][capacity : 2 * capacity, :]
    users_copy.wait()
    place = own_placement(users, me, peers, capacity)
    out_ref[...] = matmul(place, held[...], ROWS_BY_ROWS).astype(BF16)


def swap(array, axis, size, bits):
    return lax.ppermute(array, axis, [(i, i ^ bits) for i in range(size)])


def direct_body(tokens, user_of_row, proj_weight, norm_gain, grad_out):
    peers = lax.axis_size("dp")
    replicas = lax.axis_size("replica")
    rows = tokens.shape[1]
    width, columns = proj_weight.shape
    features = grad_out.shape[2]
    capacity = 2 * rows // peers
    slots = peers * capacity
    chips = peers // 2
    block = width // peers
    half = block // 2
    size = columns // 2
    users = user_of_row.reshape(peers, rows)
    gain = norm_gain.reshape(1, features)
    exchange = functools.partial(swap, axis="dp", size=peers)
    swap_replicas = functools.partial(swap, axis="replica", size=replicas)
    pair = shaped((2 * capacity, width), BF16)
    users_scratch = pltpu.VMEM((peers, rows), jnp.int32)

    def to_sources(pairs):
        return [pairs[0]] + [exchange(pairs[i], bits=2 * i) for i in range(1, chips)]

    def to_siblings(pairs):
        return [exchange(a, bits=1) for a in pairs]

    packed = call(
        functools.partial(pack_kernel, peers, capacity),
        [pair] * chips,
        [users, tokens[0]],
        2 * slots * rows * width,
        [users_scratch, pltpu.VMEM((rows, width), BF16), pltpu.SemaphoreType.DMA((2,))],
        [HBM, HBM],
    )
    near = to_sources(packed)
    w_held, grad, code, key = call(
        functools.partial(prep_kernel, peers, capacity),
        [
            shaped((width, columns), BF16),
            shaped((slots, features), F32),
            shaped((slots, HEAD_DIM), F32),
            shaped((8, slots), F32),
        ],
        [users, gain, proj_weight, grad_out[0]],
        2 * slots * slots * rows,
        [users_scratch, pltpu.VMEM((slots, features), BF16), pltpu.SemaphoreType.DMA((3,))],
        [HBM, VMEM, HBM, HBM],
    )
    near, (w_held, grad, code, key) = lax.optimization_barrier((near, (w_held, grad, code, key)))
    far = to_siblings(near)
    attended, d_first, d_second, x_own, x_sib = call(
        functools.partial(attend_kernel, peers, capacity, peers * rows),
        [shaped((slots, features), BF16)] + [shaped((slots, size), BF16)] * 2 + [shaped((slots, width // 2), BF16)] * 2,
        [gain, w_held, grad, code, key, *near, *far],
        2 * slots * width * columns + 14 * slots * slots * features,
        [
            pltpu.VMEM((slots, width), BF16),
            pltpu.VMEM((slots, width), BF16),
            pltpu.VMEM((slots, columns), BF16),
            pltpu.VMEM((slots, columns), F32),
        ],
    )
    flops = 4 * slots * (width // 2) * size
    own, *others = call(
        weight_kernel,
        [shaped((block, size), F32)] + [shaped((block, size), BF16)] * (chips - 1),
        [x_own, x_sib, d_first, exchange(d_first, bits=1)],
        flops,
    )
    keep_second, send_second = call(
        functools.partial(weight_halves_kernel, chips),
        [shaped((chips * half, size), F32), shaped((chips * half, size), BF16)],
        [x_own, x_sib, d_second, exchange(d_second, bits=1)],
        flops,
        [pltpu.VMEM((block, size), F32)],
    )
    from_plane = [exchange(other, bits=2 * (i + 1)) for i, other in enumerate(others)]
    from_neighbour = swap_replicas(send_second, bits=1)
    keep_first, send_first = call(
        sum_halves_kernel,
        [shaped((half, size), F32), shaped((half, size), BF16)],
        [own, *from_plane],
        chips * block * size,
        [pltpu.VMEM((block, size), F32)],
    )
    own_second, *others_second = call(
        sum_blocks_kernel,
        [shaped((half, size), F32)] + [shaped((half, size), BF16)] * (chips - 1),
        [keep_second, from_neighbour],
        chips * half * size,
    )
    first = keep_first + swap_replicas(send_first, bits=1).astype(F32)
    second = own_second
    for i, other in enumerate(others_second):
        second = second + exchange(other, bits=2 * (i + 1)).astype(F32)
    d_slots = call(
        functools.partial(token_kernel, features),
        [pair] * chips,
        [w_held, d_first, d_second],
        2 * slots * width * columns,
    )
    d_slots, second = lax.optimization_barrier((d_slots, second))
    near = to_sources(d_slots)
    far = to_siblings(near)
    (grad_tokens,) = call(
        functools.partial(unpack_kernel, peers, capacity),
        [shaped((rows, width), BF16)],
        [users, *near, *far],
        2 * slots * rows * width,
        [pltpu.VMEM((slots, width), BF16), users_scratch, pltpu.SemaphoreType.DMA((1,))],
        [HBM] + [VMEM] * (2 * chips),
    )
    joined = []
    for total in (first, second):
        held = total.astype(BF16)
        bits = 2
        while bits < replicas:
            held = (held.astype(F32) + swap_replicas(held, bits=bits).astype(F32)).astype(BF16)
            bits *= 2
        joined += [held, swap_replicas(held, bits=1)]
    (grad_weight,) = call(
        functools.partial(join_kernel, features),
        [shaped((block, columns), F32)],
        joined,
        block * columns,
    )

    return (attended[None], grad_tokens[None], grad_weight)


def power_of_two(value):
    return value > 1 and value & (value - 1) == 0


def body(tokens, user_of_row, proj_weight, norm_gain, grad_out):
    peers = lax.axis_size("dp")
    replicas = lax.axis_size("replica")
    capacity = 2 * tokens.shape[1] // peers
    aligned = capacity % 16 == 0 and proj_weight.shape[0] // peers % 128 == 0
    run = direct_body if aligned and power_of_two(peers) and power_of_two(replicas) else general_body
    return run(tokens, user_of_row, proj_weight, norm_gain, grad_out)


def solution(mesh):
    return jax.shard_map(
        body,
        mesh=mesh,
        in_specs=(P("replica", "dp", None), P("replica", None), P(), P(), P("replica", "dp", None)),
        out_specs=(P("replica", "dp", None), P("replica", "dp", None), P("dp", None)),
        check_vma=False,
    )
```

```python
import functools

import jax
import jax.numpy as jnp
from jax import lax
from jax.experimental import pallas as pl
from jax.experimental.pallas import tpu as pltpu
from jax.sharding import PartitionSpec as P

HEADS = 4
HEAD_DIM = 128
UPO = 4


def silu_grad(preact):
    sigmoid_p = jax.nn.sigmoid(preact)
    return sigmoid_p * (1.0 + preact * (1.0 - sigmoid_p))


def attend(activated, gain, slot_user, slot_order):
    slot_total = activated.shape[0]
    split_acts = activated.astype(jnp.float32).reshape(slot_total, 3, HEADS, HEAD_DIM)
    queries = split_acts[:, 0]
    keys_h = split_acts[:, 1]
    values = split_acts[:, 2]
    scores = jnp.einsum(
        "qhd,khd->hqk", queries, keys_h, precision=lax.Precision.HIGHEST
    ) * HEAD_DIM ** (-0.5)
    visible = (
        (slot_user[:, None] == slot_user[None, :])
        & (slot_order[None, :] <= slot_order[:, None])
        & (slot_user[:, None] >= 0)
    )
    weights = jnp.where(visible[None], jax.nn.silu(scores), 0.0)
    mixed = jnp.einsum("hqk,khd->qhd", weights, values, precision=lax.Precision.HIGHEST).reshape(
        slot_total, HEADS * HEAD_DIM
    )
    mean_row = jnp.mean(mixed, axis=1, keepdims=True)
    centered = mixed - mean_row
    variance = jnp.mean(centered * centered, axis=1, keepdims=True)
    return centered * lax.rsqrt(variance + 1e-06) * gain


def block_pass(activated, gain, slot_user, slot_order, cotangent):

    def forward(acts):
        return attend(acts, gain, slot_user, slot_order)

    normed, pull = jax.vjp(forward, activated)
    (d_acts,) = pull(cotangent.astype(jnp.float32))
    return (normed.astype(jnp.bfloat16), d_acts)


def general_body(tokens, user_of_row, proj_weight, norm_gain, grad_out):
    peer_count = lax.axis_size("dp")
    self_index = lax.axis_index("dp")
    row_count = tokens.shape[1]
    width = proj_weight.shape[0]
    capacity = 2 * row_count // peer_count
    slot_count = peer_count * capacity
    routing = user_of_row[0]
    owners = (routing // UPO).reshape(peer_count, row_count)
    peer_ids = jnp.arange(peer_count, dtype=jnp.int32)
    inbound = (owners == self_index).astype(jnp.int32)
    in_rank = jnp.cumsum(inbound, axis=1) - 1
    matches = (
        (inbound[:, None, :] == 1)
        & (in_rank[:, None, :] == jnp.arange(capacity, dtype=jnp.int32)[None, :, None])
    ).astype(jnp.int32)
    users_src = routing.reshape(peer_count, row_count)
    slot_user = jnp.sum(matches * (users_src[:, None, :] + 1), axis=2).reshape(slot_count) - 1
    order_src = jnp.arange(peer_count * row_count, dtype=jnp.int32).reshape(peer_count, row_count)
    slot_order = jnp.sum(matches * order_src[:, None, :], axis=2).reshape(slot_count)
    own_owner = lax.dynamic_slice_in_dim(owners, self_index, 1, 0)[0]
    to_peer = (own_owner[:, None] == peer_ids[None, :]).astype(jnp.int32)
    out_rank = jnp.sum(jnp.cumsum(to_peer, axis=0) * to_peer, axis=1) - 1
    position = own_owner * capacity + out_rank
    rows_x = tokens[0]
    cotangent = grad_out[0]
    contract_cols = (((1,), (1,)), ((), ()))
    contract_rows = (((0,), (0,)), ((), ()))
    outgoing = jnp.zeros((slot_count, width), rows_x.dtype).at[position].set(rows_x)
    arrived = lax.all_to_all(outgoing, "dp", split_axis=0, concat_axis=0, tiled=True)
    preact = jnp.dot(arrived, proj_weight, preferred_element_type=jnp.float32)
    activated = jax.nn.silu(preact).astype(jnp.bfloat16)
    attended, d_acts = block_pass(activated, norm_gain, slot_user, slot_order, cotangent)
    d_acts = lax.optimization_barrier(d_acts)
    d_pre = (d_acts.astype(jnp.float32) * silu_grad(preact)).astype(jnp.bfloat16)
    d_slots = lax.dot_general(
        d_pre, proj_weight, contract_cols, preferred_element_type=jnp.float32
    ).astype(jnp.bfloat16)
    returned = lax.all_to_all(d_slots, "dp", split_axis=0, concat_axis=0, tiled=True)
    grad_tokens = returned[position]
    weight_shard = lax.psum_scatter(
        lax.dot_general(arrived, d_pre, contract_rows, preferred_element_type=jnp.float32),
        "dp",
        scatter_dimension=0,
        tiled=True,
    )
    grad_weight = lax.psum(weight_shard, "replica")
    return (attended[None], grad_tokens[None], grad_weight)


F32 = jnp.float32
BF16 = jnp.bfloat16
ROWS_BY_COLS = (((1,), (0,)), ((), ()))
COLS_BY_COLS = (((1,), (1,)), ((), ()))
ROWS_BY_ROWS = (((0,), (0,)), ((), ()))
VMEM_LIMIT = 32 * 1024 * 1024
HBM = pl.BlockSpec(memory_space=pltpu.HBM)
VMEM = pl.BlockSpec(memory_space=pltpu.VMEM)


def matmul(left, right, contract=ROWS_BY_COLS):
    return lax.dot_general(left, right, contract, preferred_element_type=F32)


def call(kernel, outs, operands, flops, scratch=(), specs=None):
    specs = specs or [VMEM] * len(operands)
    nbytes = sum(a.size * a.dtype.itemsize for a in operands)
    nbytes += sum(o.size * o.dtype.itemsize for o in outs)
    return pl.pallas_call(
        kernel,
        out_shape=outs,
        in_specs=specs,
        out_specs=[VMEM] * len(outs),
        scratch_shapes=list(scratch),
        compiler_params=pltpu.CompilerParams(vmem_limit_bytes=VMEM_LIMIT),
        cost_estimate=pl.CostEstimate(flops=flops, bytes_accessed=nbytes, transcendentals=0),
    )(*[pltpu.with_memory_space_constraint(a, pltpu.HBM) if s is HBM else a for a, s in zip(operands, specs)])


def shaped(shape, dtype):
    return jax.ShapeDtypeStruct(shape, dtype)


def running_count(flags):
    length = flags.shape[1]
    at = lax.broadcasted_iota(jnp.int32, (length, length), 0)
    upto = lax.broadcasted_iota(jnp.int32, (length, length), 1)
    return matmul(flags, (at <= upto).astype(F32))


def own_placement(users_ref, me, peers, capacity):
    owner = lax.div(users_ref[pl.ds(me, 1), :], UPO)
    rows = owner.shape[1]
    match = (lax.broadcasted_iota(jnp.int32, (peers, rows), 0) == owner).astype(F32)
    rank = jnp.sum(running_count(match) * match, axis=0, keepdims=True) - 1.0
    key = (owner ^ me) * capacity + rank.astype(jnp.int32)
    return (lax.broadcasted_iota(jnp.int32, (peers * capacity, rows), 0) == key).astype(BF16)


def fetch(pairs, sems):
    copies = [pltpu.make_async_copy(src, dst, sems.at[i]) for i, (src, dst) in enumerate(pairs)]
    for copy in copies:
        copy.start()
    return copies


def pack_kernel(peers, capacity, users_hbm, tokens_hbm, *refs):
    *out_refs, users, rows, sems = refs
    users_copy, rows_copy = fetch([(users_hbm, users), (tokens_hbm, rows)], sems)
    me = lax.axis_index("dp")
    users_copy.wait()
    place = own_placement(users, me, peers, capacity)
    rows_copy.wait()
    packed = matmul(place, rows[...]).astype(BF16)
    for i, out_ref in enumerate(out_refs):
        out_ref[...] = packed[2 * i * capacity : 2 * (i + 1) * capacity]


def slot_codes(users_ref, me, peers, capacity):
    users = jnp.concatenate([users_ref[pl.ds(me ^ m, 1), :] for m in range(peers)], axis=0)
    rows = users.shape[1]
    match = (lax.div(users, UPO) == me).astype(F32)
    rank = running_count(match) * match - 1.0
    position = lax.broadcasted_iota(jnp.int32, (1, rows), 1)
    slot = lax.broadcasted_iota(jnp.int32, (capacity, rows), 0).astype(F32)
    codes = []
    for m in range(peers):
        code = (users[m : m + 1] + 1) * (peers * rows) + (me ^ m) * rows + position
        picked = jnp.where(rank[m : m + 1] == slot, code.astype(F32), 0.0)
        codes.append(jnp.sum(picked, axis=1, keepdims=True))
    return jnp.concatenate(codes, axis=0)


def prep_kernel(peers, capacity, users_hbm, gain_ref, w_hbm, grad_hbm, w_ref, grad_ref, code_ref, key_ref, users, grad, sems):
    users_copy, grad_copy, w_copy = fetch([(users_hbm, users), (grad_hbm, grad), (w_hbm, w_ref)], sems)
    me = lax.axis_index("dp")
    users_copy.wait()
    code = jnp.broadcast_to(slot_codes(users, me, peers, capacity), code_ref.shape)
    code_ref[...] = code
    key_ref[...] = code.T[0 : key_ref.shape[0]]
    grad_copy.wait()
    for m in range(peers):
        at = pl.multiple_of((me ^ m) * capacity, capacity)
        grad_ref[m * capacity : (m + 1) * capacity, :] = grad[pl.ds(at, capacity), :].astype(F32) * gain_ref[...]
    w_copy.wait()


def attend_kernel(peers, capacity, batch_rows, gain_ref, w_ref, grad, code_ref, key_ref, *refs):
    chips = peers // 2
    near, far, refs = refs[:chips], refs[chips : 2 * chips], refs[2 * chips :]
    attended_ref, *d_refs, x_own_ref, x_sib_ref, x, x_sib, act, slope = refs
    me = lax.axis_index("dp")
    slots = peers * capacity
    width, columns = w_ref.shape
    features = gain_ref.shape[1]
    block = width // peers
    first, second = slice(0, capacity), slice(capacity, 2 * capacity)
    for i in range(chips):
        even = slice(2 * i * capacity, (2 * i + 1) * capacity)
        odd = slice((2 * i + 1) * capacity, (2 * i + 2) * capacity)
        x[even, :] = near[i][first, :]
        x[odd, :] = far[i][second, :]
        x_sib[even, :] = far[i][first, :]
        x_sib[odd, :] = near[i][second, :]
    for i in range(chips):
        at = pl.multiple_of((me ^ (2 * i)) * block, block)
        x_own_ref[:, i * block : (i + 1) * block] = x[:, pl.ds(at, block)]
        x_sib_ref[:, i * block : (i + 1) * block] = x_sib[:, pl.ds(at, block)]
    gain = gain_ref[...]
    step = 2 * HEAD_DIM
    for c in range(0, columns, step):
        preact = matmul(x[...], w_ref[:, c : c + step])
        gate = 0.5 * jnp.tanh(0.5 * preact) + 0.5
        silu = preact * gate
        act[:, c : c + step] = silu.astype(BF16)
        slope[:, c : c + step] = gate + silu * (1.0 - gate)

    code = code_ref[:, 0:1]
    code_of_key = key_ref[0:1, :]
    first = (lax.div(code.astype(jnp.int32), batch_rows) * batch_rows).astype(F32)
    first = jnp.where(code > 0.0, first, code + 1.0)
    visible = (code_of_key <= code) & (code_of_key >= first)

    def head(base, h):
        return act[:, base + h * HEAD_DIM : base + (h + 1) * HEAD_DIM]

    scale = HEAD_DIM**-0.5
    weights, slopes, mixed = [], [], []
    for h in range(HEADS):
        scores = matmul(head(0, h), head(features, h), COLS_BY_COLS) * scale
        gate = 0.5 * jnp.tanh(0.5 * scores) + 0.5
        silu = scores * gate
        weight = jnp.where(visible, silu, 0.0).astype(BF16)
        slopes.append(jnp.where(visible, (gate + silu * (1.0 - gate)) * scale, 0.0))
        weights.append(weight)
        mixed.append(matmul(weight, head(2 * features, h)))
    mean = sum(jnp.sum(v, axis=1, keepdims=True) for v in mixed) / features
    centered = [v - mean for v in mixed]
    variance = sum(jnp.sum(v * v, axis=1, keepdims=True) for v in centered) / features
    inverse = lax.rsqrt(variance + 1e-06)
    unit = [v * inverse for v in centered]

    def part(ref, h):
        return ref[:, h * HEAD_DIM : (h + 1) * HEAD_DIM]

    grads = [part(grad, h) for h in range(HEADS)]
    for h in range(HEADS):
        normed = (unit[h] * part(gain, h)).astype(BF16)
        for m in range(peers):
            at = pl.multiple_of((me ^ m) * capacity, capacity)
            attended_ref[pl.ds(at, capacity), h * HEAD_DIM : (h + 1) * HEAD_DIM] = normed[m * capacity : (m + 1) * capacity]
    grad_mean = sum(jnp.sum(g, axis=1, keepdims=True) for g in grads) / features
    grad_unit = sum(jnp.sum(g * u, axis=1, keepdims=True) for g, u in zip(grads, unit)) / features
    per = HEADS // len(d_refs)
    for h in range(HEADS):
        d_ref, at = d_refs[h // per], (h % per) * HEAD_DIM
        d_mixed = ((grads[h] - grad_mean - unit[h] * grad_unit) * inverse).astype(BF16)
        d_scores = (matmul(d_mixed, head(2 * features, h), COLS_BY_COLS) * slopes[h]).astype(BF16)
        d_query = matmul(d_scores, head(features, h))
        d_key = matmul(d_scores, head(0, h), ROWS_BY_ROWS)
        d_value = matmul(weights[h], d_mixed, ROWS_BY_ROWS)
        for j, d in enumerate((d_query, d_key, d_value)):
            to = j * per * HEAD_DIM + at
            d_ref[:, to : to + HEAD_DIM] = (d * part(slope, j * HEADS + h)).astype(BF16)


def weight_block(i, x_own_ref, x_sib_ref, d_own_ref, d_sib_ref, block):
    at = slice(i * block, (i + 1) * block)
    total = matmul(x_own_ref[:, at], d_own_ref[...], ROWS_BY_ROWS)
    return total + matmul(x_sib_ref[:, at], d_sib_ref[...], ROWS_BY_ROWS)


def weight_kernel(x_own_ref, x_sib_ref, d_own_ref, d_sib_ref, *out_refs):
    block = x_own_ref.shape[1] // len(out_refs)
    for i, out_ref in enumerate(out_refs):
        out_ref[...] = weight_block(i, x_own_ref, x_sib_ref, d_own_ref, d_sib_ref, block).astype(out_ref.dtype)


def halves(half):
    side = lax.rem(lax.axis_index("replica"), 2)
    return pl.multiple_of(side * half, half), pl.multiple_of((1 - side) * half, half)


def weight_halves_kernel(blocks, x_own_ref, x_sib_ref, d_own_ref, d_sib_ref, keep_ref, send_ref, held):
    block = held.shape[0]
    half = block // 2
    keep_at, send_at = halves(half)
    for i in range(blocks):
        held[...] = weight_block(i, x_own_ref, x_sib_ref, d_own_ref, d_sib_ref, block)
        rows = slice(i * half, (i + 1) * half)
        keep_ref[rows, :] = held[pl.ds(keep_at, half), :]
        send_ref[rows, :] = held[pl.ds(send_at, half), :].astype(BF16)


def sum_halves_kernel(own_ref, *refs):
    *in_refs, keep_ref, send_ref, held = refs
    half = held.shape[0] // 2
    total = own_ref[...]
    for in_ref in in_refs:
        total = total + in_ref[...].astype(F32)
    held[...] = total
    keep_at, send_at = halves(half)
    keep_ref[...] = held[pl.ds(keep_at, half), :]
    send_ref[...] = held[pl.ds(send_at, half), :].astype(BF16)


def sum_blocks_kernel(keep_ref, in_ref, *out_refs):
    half = out_refs[0].shape[0]
    for i, out_ref in enumerate(out_refs):
        rows = slice(i * half, (i + 1) * half)
        out_ref[...] = (keep_ref[rows, :] + in_ref[rows, :].astype(F32)).astype(out_ref.dtype)


def join_kernel(features, *refs):
    *in_refs, out_ref = refs
    half, size = in_refs[0].shape
    keep_at, send_at = halves(half)
    per = size // 3
    for p in range(len(in_refs) // 2):
        for in_ref, at in ((in_refs[2 * p], keep_at), (in_refs[2 * p + 1], send_at)):
            for j in range(3):
                to = j * features + p * per
                out_ref[pl.ds(at, half), to : to + per] = in_ref[:, j * per : (j + 1) * per].astype(F32)


def token_kernel(features, w_ref, *refs):
    d_refs, out_refs = refs[:2], refs[2:]
    rows = out_refs[0].shape[0]
    per = d_refs[0].shape[1] // 3
    total = None
    for p, d_ref in enumerate(d_refs):
        for j in range(3):
            at = j * features + p * per
            term = matmul(d_ref[:, j * per : (j + 1) * per], w_ref[:, at : at + per], COLS_BY_COLS)
            total = term if total is None else total + term
    for i, out_ref in enumerate(out_refs):
        out_ref[...] = total[i * rows : (i + 1) * rows].astype(BF16)


def unpack_kernel(peers, capacity, users_hbm, *refs):
    chips = peers // 2
    near, far, (out_ref, held, users, sems) = refs[:chips], refs[chips : 2 * chips], refs[2 * chips :]
    (users_copy,) = fetch([(users_hbm, users)], sems)
    me = lax.axis_index("dp")
    for i in range(chips):
        held[2 * i * capacity : (2 * i + 1) * capacity, :] = near[i][0:capacity, :]
        held[(2 * i + 1) * capacity : (2 * i + 2) * capacity, :] = far[i][capacity : 2 * capacity, :]
    users_copy.wait()
    place = own_placement(users, me, peers, capacity)
    out_ref[...] = matmul(place, held[...], ROWS_BY_ROWS).astype(BF16)


def swap(array, axis, size, bits):
    return lax.ppermute(array, axis, [(i, i ^ bits) for i in range(size)])


def direct_body(tokens, user_of_row, proj_weight, norm_gain, grad_out):
    peers = lax.axis_size("dp")
    replicas = lax.axis_size("replica")
    rows = tokens.shape[1]
    width, columns = proj_weight.shape
    features = grad_out.shape[2]
    capacity = 2 * rows // peers
    slots = peers * capacity
    chips = peers // 2
    block = width // peers
    half = block // 2
    size = columns // 2
    users = user_of_row.reshape(peers, rows)
    gain = norm_gain.reshape(1, features)
    exchange = functools.partial(swap, axis="dp", size=peers)
    swap_replicas = functools.partial(swap, axis="replica", size=replicas)
    pair = shaped((2 * capacity, width), BF16)
    users_scratch = pltpu.VMEM((peers, rows), jnp.int32)

    def farthest_first(arrays):
        sent = [exchange(arrays[i], bits=2 * (i + 1)) for i in reversed(range(chips - 1))]
        return sent[::-1]

    def to_sources(pairs):
        return [pairs[0]] + farthest_first(pairs[1:])

    def to_siblings(pairs):
        return [exchange(a, bits=1) for a in pairs]

    packed = call(
        functools.partial(pack_kernel, peers, capacity),
        [pair] * chips,
        [users, tokens[0]],
        2 * slots * rows * width,
        [users_scratch, pltpu.VMEM((rows, width), BF16), pltpu.SemaphoreType.DMA((2,))],
        [HBM, HBM],
    )
    near = to_sources(packed)
    w_held, grad, code, key = call(
        functools.partial(prep_kernel, peers, capacity),
        [
            shaped((width, columns), BF16),
            shaped((slots, features), F32),
            shaped((slots, HEAD_DIM), F32),
            shaped((8, slots), F32),
        ],
        [users, gain, proj_weight, grad_out[0]],
        2 * slots * slots * rows,
        [users_scratch, pltpu.VMEM((slots, features), BF16), pltpu.SemaphoreType.DMA((3,))],
        [HBM, VMEM, HBM, HBM],
    )
    near, (w_held, grad, code, key) = lax.optimization_barrier((near, (w_held, grad, code, key)))
    far = to_siblings(near)
    attended, d_first, d_second, x_own, x_sib = call(
        functools.partial(attend_kernel, peers, capacity, peers * rows),
        [shaped((slots, features), BF16)] + [shaped((slots, size), BF16)] * 2 + [shaped((slots, width // 2), BF16)] * 2,
        [gain, w_held, grad, code, key, *near, *far],
        2 * slots * width * columns + 14 * slots * slots * features,
        [
            pltpu.VMEM((slots, width), BF16),
            pltpu.VMEM((slots, width), BF16),
            pltpu.VMEM((slots, columns), BF16),
            pltpu.VMEM((slots, columns), F32),
        ],
    )
    flops = 4 * slots * (width // 2) * size
    own, *others = call(
        weight_kernel,
        [shaped((block, size), F32)] + [shaped((block, size), BF16)] * (chips - 1),
        [x_own, x_sib, d_first, exchange(d_first, bits=1)],
        flops,
    )
    keep_second, send_second = call(
        functools.partial(weight_halves_kernel, chips),
        [shaped((chips * half, size), F32), shaped((chips * half, size), BF16)],
        [x_own, x_sib, d_second, exchange(d_second, bits=1)],
        flops,
        [pltpu.VMEM((block, size), F32)],
    )
    from_plane = farthest_first(others)
    from_neighbour = swap_replicas(send_second, bits=1)
    own_second, *others_second = call(
        sum_blocks_kernel,
        [shaped((half, size), F32)] + [shaped((half, size), BF16)] * (chips - 1),
        [keep_second, from_neighbour],
        chips * half * size,
    )
    second_plane = farthest_first(others_second)
    from_plane, own_second = lax.optimization_barrier((from_plane, own_second))
    keep_first, send_first = call(
        sum_halves_kernel,
        [shaped((half, size), F32), shaped((half, size), BF16)],
        [own, *from_plane],
        chips * block * size,
        [pltpu.VMEM((block, size), F32)],
    )
    first = keep_first + swap_replicas(send_first, bits=1).astype(F32)
    second = own_second
    for other in second_plane:
        second = second + other.astype(F32)
    d_slots = call(
        functools.partial(token_kernel, features),
        [pair] * chips,
        [w_held, d_first, d_second],
        2 * slots * width * columns,
    )
    d_slots, _, _ = lax.optimization_barrier((d_slots, first.astype(BF16), second.astype(BF16)))
    near = to_sources(d_slots)
    far = to_siblings(near)
    (grad_tokens,) = call(
        functools.partial(unpack_kernel, peers, capacity),
        [shaped((rows, width), BF16)],
        [users, *near, *far],
        2 * slots * rows * width,
        [pltpu.VMEM((slots, width), BF16), users_scratch, pltpu.SemaphoreType.DMA((1,))],
        [HBM] + [VMEM] * (2 * chips),
    )
    joined = []
    for total in (first, second):
        held = total.astype(BF16)
        bits = 2
        while bits < replicas:
            held = (held.astype(F32) + swap_replicas(held, bits=bits).astype(F32)).astype(BF16)
            bits *= 2
        joined += [held, swap_replicas(held, bits=1)]
    joined[-1], grad_tokens = lax.optimization_barrier((joined[-1], grad_tokens))
    (grad_weight,) = call(
        functools.partial(join_kernel, features),
        [shaped((block, columns), F32)],
        joined,
        block * columns,
    )

    return (attended[None], grad_tokens[None], grad_weight)


def power_of_two(value):
    return value > 1 and value & (value - 1) == 0


def body(tokens, user_of_row, proj_weight, norm_gain, grad_out):
    peers = lax.axis_size("dp")
    replicas = lax.axis_size("replica")
    capacity = 2 * tokens.shape[1] // peers
    aligned = capacity % 16 == 0 and proj_weight.shape[0] // peers % 128 == 0
    run = direct_body if aligned and power_of_two(peers) and power_of_two(replicas) else general_body
    return run(tokens, user_of_row, proj_weight, norm_gain, grad_out)


def solution(mesh):
    return jax.shard_map(
        body,
        mesh=mesh,
        in_specs=(P("replica", "dp", None), P("replica", None), P(), P(), P("replica", "dp", None)),
        out_specs=(P("replica", "dp", None), P("replica", "dp", None), P("dp", None)),
        check_vma=False,
    )
```

```python
import functools

import jax
import jax.numpy as jnp
from jax import lax
from jax.experimental import pallas as pl
from jax.experimental.pallas import tpu as pltpu
from jax.sharding import PartitionSpec as P

HEADS = 4
HEAD_DIM = 128
UPO = 4


def silu_grad(preact):
    sigmoid_p = jax.nn.sigmoid(preact)
    return sigmoid_p * (1.0 + preact * (1.0 - sigmoid_p))


def attend(activated, gain, slot_user, slot_order):
    slot_total = activated.shape[0]
    split_acts = activated.astype(jnp.float32).reshape(slot_total, 3, HEADS, HEAD_DIM)
    queries = split_acts[:, 0]
    keys_h = split_acts[:, 1]
    values = split_acts[:, 2]
    scores = jnp.einsum(
        "qhd,khd->hqk", queries, keys_h, precision=lax.Precision.HIGHEST
    ) * HEAD_DIM ** (-0.5)
    visible = (
        (slot_user[:, None] == slot_user[None, :])
        & (slot_order[None, :] <= slot_order[:, None])
        & (slot_user[:, None] >= 0)
    )
    weights = jnp.where(visible[None], jax.nn.silu(scores), 0.0)
    mixed = jnp.einsum("hqk,khd->qhd", weights, values, precision=lax.Precision.HIGHEST).reshape(
        slot_total, HEADS * HEAD_DIM
    )
    mean_row = jnp.mean(mixed, axis=1, keepdims=True)
    centered = mixed - mean_row
    variance = jnp.mean(centered * centered, axis=1, keepdims=True)
    return centered * lax.rsqrt(variance + 1e-06) * gain


def block_pass(activated, gain, slot_user, slot_order, cotangent):

    def forward(acts):
        return attend(acts, gain, slot_user, slot_order)

    normed, pull = jax.vjp(forward, activated)
    (d_acts,) = pull(cotangent.astype(jnp.float32))
    return (normed.astype(jnp.bfloat16), d_acts)


def general_body(tokens, user_of_row, proj_weight, norm_gain, grad_out):
    peer_count = lax.axis_size("dp")
    self_index = lax.axis_index("dp")
    row_count = tokens.shape[1]
    width = proj_weight.shape[0]
    capacity = 2 * row_count // peer_count
    slot_count = peer_count * capacity
    routing = user_of_row[0]
    owners = (routing // UPO).reshape(peer_count, row_count)
    peer_ids = jnp.arange(peer_count, dtype=jnp.int32)
    inbound = (owners == self_index).astype(jnp.int32)
    in_rank = jnp.cumsum(inbound, axis=1) - 1
    matches = (
        (inbound[:, None, :] == 1)
        & (in_rank[:, None, :] == jnp.arange(capacity, dtype=jnp.int32)[None, :, None])
    ).astype(jnp.int32)
    users_src = routing.reshape(peer_count, row_count)
    slot_user = jnp.sum(matches * (users_src[:, None, :] + 1), axis=2).reshape(slot_count) - 1
    order_src = jnp.arange(peer_count * row_count, dtype=jnp.int32).reshape(peer_count, row_count)
    slot_order = jnp.sum(matches * order_src[:, None, :], axis=2).reshape(slot_count)
    own_owner = lax.dynamic_slice_in_dim(owners, self_index, 1, 0)[0]
    to_peer = (own_owner[:, None] == peer_ids[None, :]).astype(jnp.int32)
    out_rank = jnp.sum(jnp.cumsum(to_peer, axis=0) * to_peer, axis=1) - 1
    position = own_owner * capacity + out_rank
    rows_x = tokens[0]
    cotangent = grad_out[0]
    contract_cols = (((1,), (1,)), ((), ()))
    contract_rows = (((0,), (0,)), ((), ()))
    outgoing = jnp.zeros((slot_count, width), rows_x.dtype).at[position].set(rows_x)
    arrived = lax.all_to_all(outgoing, "dp", split_axis=0, concat_axis=0, tiled=True)
    preact = jnp.dot(arrived, proj_weight, preferred_element_type=jnp.float32)
    activated = jax.nn.silu(preact).astype(jnp.bfloat16)
    attended, d_acts = block_pass(activated, norm_gain, slot_user, slot_order, cotangent)
    d_acts = lax.optimization_barrier(d_acts)
    d_pre = (d_acts.astype(jnp.float32) * silu_grad(preact)).astype(jnp.bfloat16)
    d_slots = lax.dot_general(
        d_pre, proj_weight, contract_cols, preferred_element_type=jnp.float32
    ).astype(jnp.bfloat16)
    returned = lax.all_to_all(d_slots, "dp", split_axis=0, concat_axis=0, tiled=True)
    grad_tokens = returned[position]
    weight_shard = lax.psum_scatter(
        lax.dot_general(arrived, d_pre, contract_rows, preferred_element_type=jnp.float32),
        "dp",
        scatter_dimension=0,
        tiled=True,
    )
    grad_weight = lax.psum(weight_shard, "replica")
    return (attended[None], grad_tokens[None], grad_weight)


F32 = jnp.float32
BF16 = jnp.bfloat16
ROWS_BY_COLS = (((1,), (0,)), ((), ()))
COLS_BY_COLS = (((1,), (1,)), ((), ()))
ROWS_BY_ROWS = (((0,), (0,)), ((), ()))
VMEM_LIMIT = 32 * 1024 * 1024
HBM = pl.BlockSpec(memory_space=pltpu.HBM)
VMEM = pl.BlockSpec(memory_space=pltpu.VMEM)


def matmul(left, right, contract=ROWS_BY_COLS):
    return lax.dot_general(left, right, contract, preferred_element_type=F32)


def call(kernel, outs, operands, flops, scratch=(), specs=None):
    specs = specs or [VMEM] * len(operands)
    nbytes = sum(a.size * a.dtype.itemsize for a in operands)
    nbytes += sum(o.size * o.dtype.itemsize for o in outs)
    return pl.pallas_call(
        kernel,
        out_shape=outs,
        in_specs=specs,
        out_specs=[VMEM] * len(outs),
        scratch_shapes=list(scratch),
        compiler_params=pltpu.CompilerParams(vmem_limit_bytes=VMEM_LIMIT),
        cost_estimate=pl.CostEstimate(flops=flops, bytes_accessed=nbytes, transcendentals=0),
    )(*[pltpu.with_memory_space_constraint(a, pltpu.HBM) if s is HBM else a for a, s in zip(operands, specs)])


def shaped(shape, dtype):
    return jax.ShapeDtypeStruct(shape, dtype)


def running_count(flags):
    length = flags.shape[1]
    at = lax.broadcasted_iota(jnp.int32, (length, length), 0)
    upto = lax.broadcasted_iota(jnp.int32, (length, length), 1)
    return matmul(flags, (at <= upto).astype(F32))


def own_placement(users_ref, me, peers, capacity, paired):
    owner = lax.div(users_ref[pl.ds(me, 1), :], UPO)
    rows = owner.shape[1]
    match = (lax.broadcasted_iota(jnp.int32, (peers, rows), 0) == owner).astype(F32)
    rank = jnp.sum(running_count(match) * match, axis=0, keepdims=True) - 1.0
    block = owner ^ me
    if not paired:
        block = lax.div(block, 2) + lax.rem(block, 2) * (peers // 2)
    key = block * capacity + rank.astype(jnp.int32)
    return (lax.broadcasted_iota(jnp.int32, (peers * capacity, rows), 0) == key).astype(BF16)


def block_order(peers):
    return [*range(0, peers, 2), *range(1, peers, 2)]


def fetch(pairs, sems):
    copies = [pltpu.make_async_copy(src, dst, sems.at[i]) for i, (src, dst) in enumerate(pairs)]
    for copy in copies:
        copy.start()
    return copies


def pack_kernel(peers, capacity, users_hbm, tokens_hbm, *refs):
    *out_refs, users, rows, sems = refs
    users_copy, rows_copy = fetch([(users_hbm, users), (tokens_hbm, rows)], sems)
    me = lax.axis_index("dp")
    users_copy.wait()
    place = own_placement(users, me, peers, capacity, True)
    rows_copy.wait()
    packed = matmul(place, rows[...]).astype(BF16)
    for i, out_ref in enumerate(out_refs):
        out_ref[...] = packed[2 * i * capacity : 2 * (i + 1) * capacity]


def sort_kernel(*refs):
    *in_refs, mine_ref, other_ref = refs
    capacity = in_refs[0].shape[0] // 2
    for i, in_ref in enumerate(in_refs):
        rows = slice(i * capacity, (i + 1) * capacity)
        mine_ref[rows, :] = in_ref[:capacity, :]
        other_ref[rows, :] = in_ref[capacity:, :]


def slot_codes(users_ref, me, peers, capacity):
    order = block_order(peers)
    users = jnp.concatenate([users_ref[pl.ds(me ^ m, 1), :] for m in order], axis=0)
    rows = users.shape[1]
    match = (lax.div(users, UPO) == me).astype(F32)
    rank = running_count(match) * match - 1.0
    position = lax.broadcasted_iota(jnp.int32, (1, rows), 1)
    slot = lax.broadcasted_iota(jnp.int32, (capacity, rows), 0).astype(F32)
    codes = []
    for i, m in enumerate(order):
        code = (users[i : i + 1] + 1) * (peers * rows) + (me ^ m) * rows + position
        picked = jnp.where(rank[i : i + 1] == slot, code.astype(F32), 0.0)
        codes.append(jnp.sum(picked, axis=1, keepdims=True))
    return jnp.concatenate(codes, axis=0)


def prep_kernel(peers, capacity, users_hbm, gain_ref, w_hbm, grad_hbm, w_ref, grad_ref, code_ref, key_ref, users, grad, sems):
    users_copy, grad_copy, w_copy = fetch([(users_hbm, users), (grad_hbm, grad), (w_hbm, w_ref)], sems)
    me = lax.axis_index("dp")
    users_copy.wait()
    code = jnp.broadcast_to(slot_codes(users, me, peers, capacity), code_ref.shape)
    code_ref[...] = code
    key_ref[...] = code.T[0 : key_ref.shape[0]]
    grad_copy.wait()
    for i, m in enumerate(block_order(peers)):
        at = pl.multiple_of((me ^ m) * capacity, capacity)
        grad_ref[i * capacity : (i + 1) * capacity, :] = grad[pl.ds(at, capacity), :].astype(F32) * gain_ref[...]
    w_copy.wait()


def attend_kernel(peers, capacity, batch_rows, gain_ref, w_ref, grad, code_ref, key_ref, near_ref, far_ref, *refs):
    attended_ref, *d_refs, x_own_ref, x, act, slope = refs
    me = lax.axis_index("dp")
    slots = peers * capacity
    width, columns = w_ref.shape
    features = gain_ref.shape[1]
    block = width // peers
    x[: slots // 2, :] = near_ref[...]
    x[slots // 2 :, :] = far_ref[...]
    for i in range(peers // 2):
        at = pl.multiple_of((me ^ (2 * i)) * block, block)
        x_own_ref[:, i * block : (i + 1) * block] = x[:, pl.ds(at, block)]
    gain = gain_ref[...]
    step = 2 * HEAD_DIM
    for c in range(0, columns, step):
        preact = matmul(x[...], w_ref[:, c : c + step])
        gate = 0.5 * jnp.tanh(0.5 * preact) + 0.5
        silu = preact * gate
        act[:, c : c + step] = silu.astype(BF16)
        slope[:, c : c + step] = gate + silu * (1.0 - gate)

    code = code_ref[:, 0:1]
    code_of_key = key_ref[0:1, :]
    first = (lax.div(code.astype(jnp.int32), batch_rows) * batch_rows).astype(F32)
    first = jnp.where(code > 0.0, first, code + 1.0)
    visible = (code_of_key <= code) & (code_of_key >= first)

    def head(base, h):
        return act[:, base + h * HEAD_DIM : base + (h + 1) * HEAD_DIM]

    scale = HEAD_DIM**-0.5
    weights, slopes, mixed = [], [], []
    for h in range(HEADS):
        scores = matmul(head(0, h), head(features, h), COLS_BY_COLS) * scale
        gate = 0.5 * jnp.tanh(0.5 * scores) + 0.5
        silu = scores * gate
        weight = jnp.where(visible, silu, 0.0).astype(BF16)
        slopes.append(jnp.where(visible, (gate + silu * (1.0 - gate)) * scale, 0.0))
        weights.append(weight)
        mixed.append(matmul(weight, head(2 * features, h)))
    mean = sum(jnp.sum(v, axis=1, keepdims=True) for v in mixed) / features
    centered = [v - mean for v in mixed]
    variance = sum(jnp.sum(v * v, axis=1, keepdims=True) for v in centered) / features
    inverse = lax.rsqrt(variance + 1e-06)
    unit = [v * inverse for v in centered]

    def part(ref, h):
        return ref[:, h * HEAD_DIM : (h + 1) * HEAD_DIM]

    grads = [part(grad, h) for h in range(HEADS)]
    for h in range(HEADS):
        normed = (unit[h] * part(gain, h)).astype(BF16)
        for i, m in enumerate(block_order(peers)):
            at = pl.multiple_of((me ^ m) * capacity, capacity)
            attended_ref[pl.ds(at, capacity), h * HEAD_DIM : (h + 1) * HEAD_DIM] = normed[i * capacity : (i + 1) * capacity]
    grad_mean = sum(jnp.sum(g, axis=1, keepdims=True) for g in grads) / features
    grad_unit = sum(jnp.sum(g * u, axis=1, keepdims=True) for g, u in zip(grads, unit)) / features
    per = HEADS // len(d_refs)
    for h in range(HEADS):
        d_ref, at = d_refs[h // per], h % per * HEAD_DIM
        d_mixed = ((grads[h] - grad_mean - unit[h] * grad_unit) * inverse).astype(BF16)
        d_scores = (matmul(d_mixed, head(2 * features, h), COLS_BY_COLS) * slopes[h]).astype(BF16)
        d_query = matmul(d_scores, head(features, h))
        d_key = matmul(d_scores, head(0, h), ROWS_BY_ROWS)
        d_value = matmul(weights[h], d_mixed, ROWS_BY_ROWS)
        for j, d in enumerate((d_query, d_key, d_value)):
            to = j * per * HEAD_DIM + at
            d_ref[:, to : to + HEAD_DIM] = (d * part(slope, j * HEADS + h)).astype(BF16)


def own_weight_kernel(peers, x_ref, near_sib_ref, far_sib_ref, d_first_ref, d_second_ref, first_ref, second_ref, x_sib_ref):
    me = lax.axis_index("dp")
    block = near_sib_ref.shape[1] // peers
    half = near_sib_ref.shape[0]
    for i in range(peers // 2):
        at = pl.multiple_of((me ^ (2 * i)) * block, block)
        x_sib_ref[:half, i * block : (i + 1) * block] = near_sib_ref[:, pl.ds(at, block)]
        x_sib_ref[half:, i * block : (i + 1) * block] = far_sib_ref[:, pl.ds(at, block)]
    first_ref[...] = matmul(x_ref[...], d_first_ref[...], ROWS_BY_ROWS)
    second_ref[...] = matmul(x_ref[...], d_second_ref[...], ROWS_BY_ROWS)


def weight_block(i, own_ref, x_sib_ref, d_sib_ref, block):
    at = slice(i * block, (i + 1) * block)
    return own_ref[at, :] + matmul(x_sib_ref[:, at], d_sib_ref[...], ROWS_BY_ROWS)


def weight_kernel(own_ref, x_sib_ref, d_sib_ref, *out_refs):
    block = out_refs[0].shape[0]
    for i, out_ref in enumerate(out_refs):
        out_ref[...] = weight_block(i, own_ref, x_sib_ref, d_sib_ref, block).astype(out_ref.dtype)


def halves(half):
    side = lax.rem(lax.axis_index("replica"), 2)
    return pl.multiple_of(side * half, half), pl.multiple_of((1 - side) * half, half)


def weight_halves_kernel(blocks, own_ref, x_sib_ref, d_sib_ref, keep_ref, send_ref, held):
    block = held.shape[0]
    half = block // 2
    keep_at, send_at = halves(half)
    for i in range(blocks):
        held[...] = weight_block(i, own_ref, x_sib_ref, d_sib_ref, block)
        rows = slice(i * half, (i + 1) * half)
        keep_ref[rows, :] = held[pl.ds(keep_at, half), :]
        send_ref[rows, :] = held[pl.ds(send_at, half), :].astype(BF16)


def sum_halves_kernel(own_ref, *refs):
    *in_refs, keep_ref, send_ref, held = refs
    half = held.shape[0] // 2
    total = own_ref[...]
    for in_ref in in_refs:
        total = total + in_ref[...].astype(F32)
    held[...] = total
    keep_at, send_at = halves(half)
    keep_ref[...] = held[pl.ds(keep_at, half), :]
    send_ref[...] = held[pl.ds(send_at, half), :].astype(BF16)


def sum_blocks_kernel(keep_ref, in_ref, *out_refs):
    half = out_refs[0].shape[0]
    for i, out_ref in enumerate(out_refs):
        rows = slice(i * half, (i + 1) * half)
        out_ref[...] = (keep_ref[rows, :] + in_ref[rows, :].astype(F32)).astype(out_ref.dtype)


def join_kernel(features, *refs):
    *in_refs, out_ref = refs
    half = out_ref.shape[0] // 2
    keep_at, send_at = halves(half)
    per = in_refs[0].shape[1] // 3
    for p in range(2):
        for in_ref, at in ((in_refs[2 * p], keep_at), (in_refs[2 * p + 1], send_at)):
            for j in range(3):
                to = j * features + p * per
                out_ref[pl.ds(at, half), to : to + per] = in_ref[:, j * per : (j + 1) * per].astype(F32)


def token_kernel(features, w_ref, *refs):
    d_refs, out_refs = refs[:2], refs[2:]
    capacity = out_refs[0].shape[0] // 2
    slots = d_refs[0].shape[0]
    per = d_refs[0].shape[1] // 3
    total = None
    for p, d_ref in enumerate(d_refs):
        for j in range(3):
            at = j * features + p * per
            term = matmul(d_ref[:, j * per : (j + 1) * per], w_ref[:, at : at + per], COLS_BY_COLS)
            total = term if total is None else total + term
    for i, out_ref in enumerate(out_refs):
        for j in range(2):
            at = j * (slots // 2) + i * capacity
            out_ref[j * capacity : (j + 1) * capacity, :] = total[at : at + capacity].astype(BF16)


def unpack_kernel(peers, capacity, users_hbm, near_ref, far_ref, out_ref, held, users, sems):
    (users_copy,) = fetch([(users_hbm, users)], sems)
    me = lax.axis_index("dp")
    half = near_ref.shape[0]
    held[:half, :] = near_ref[...]
    held[half:, :] = far_ref[...]
    users_copy.wait()
    place = own_placement(users, me, peers, capacity, False)
    out_ref[...] = matmul(place, held[...], ROWS_BY_ROWS).astype(BF16)


def swap(array, axis, size, bits):
    return lax.ppermute(array, axis, [(i, i ^ bits) for i in range(size)])


def direct_body(tokens, user_of_row, proj_weight, norm_gain, grad_out):
    peers = lax.axis_size("dp")
    replicas = lax.axis_size("replica")
    rows = tokens.shape[1]
    width, columns = proj_weight.shape
    features = grad_out.shape[2]
    capacity = 2 * rows // peers
    slots = peers * capacity
    chips = peers // 2
    block = width // peers
    half = block // 2
    size = columns // 2
    users = user_of_row.reshape(peers, rows)
    gain = norm_gain.reshape(1, features)
    exchange = functools.partial(swap, axis="dp", size=peers)
    swap_replicas = functools.partial(swap, axis="replica", size=replicas)
    pair = shaped((2 * capacity, width), BF16)
    sorted_half = shaped((slots // 2, width), BF16)
    users_scratch = pltpu.VMEM((peers, rows), jnp.int32)

    def across_chips(arrays):
        return [arrays[0]] + [exchange(arrays[i], bits=2 * i) for i in range(1, chips)]

    packed = call(
        functools.partial(pack_kernel, peers, capacity),
        [pair] * chips,
        [users, tokens[0]],
        2 * slots * rows * width,
        [users_scratch, pltpu.VMEM((rows, width), BF16), pltpu.SemaphoreType.DMA((2,))],
        [HBM, HBM],
    )
    arrived = across_chips(packed)
    prepared = call(
        functools.partial(prep_kernel, peers, capacity),
        [
            shaped((width, columns), BF16),
            shaped((slots, features), F32),
            shaped((slots, HEAD_DIM), F32),
            shaped((8, slots), F32),
        ],
        [users, gain, proj_weight, grad_out[0]],
        2 * slots * slots * rows,
        [users_scratch, pltpu.VMEM((slots, features), BF16), pltpu.SemaphoreType.DMA((3,))],
        [HBM, VMEM, HBM, HBM],
    )
    arrived, (w_held, grad, code, key) = lax.optimization_barrier((arrived, prepared))
    near, far_sib = call(sort_kernel, [sorted_half] * 2, arrived, slots * width)
    far = exchange(far_sib, bits=1)
    far, near_sib = lax.optimization_barrier((far, exchange(near, bits=1)))
    attended, d_first, d_second, x_own = call(
        functools.partial(attend_kernel, peers, capacity, peers * rows),
        [shaped((slots, features), BF16)] + [shaped((slots, size), BF16)] * 2 + [shaped((slots, width // 2), BF16)],
        [gain, w_held, grad, code, key, near, far],
        2 * slots * width * columns + 14 * slots * slots * features,
        [
            pltpu.VMEM((slots, width), BF16),
            pltpu.VMEM((slots, columns), BF16),
            pltpu.VMEM((slots, columns), F32),
        ],
    )
    flops = slots * width * size
    own_first, own_second, x_sib = call(
        functools.partial(own_weight_kernel, peers),
        [shaped((width // 2, size), F32)] * 2 + [shaped((slots, width // 2), BF16)],
        [x_own, near_sib, far_sib, d_first, d_second],
        2 * flops,
    )
    own, *others = call(
        weight_kernel,
        [shaped((block, size), F32)] + [shaped((block, size), BF16)] * (chips - 1),
        [own_first, x_sib, exchange(d_first, bits=1)],
        flops,
    )
    keep_second, send_second = call(
        functools.partial(weight_halves_kernel, chips),
        [shaped((chips * half, size), F32), shaped((chips * half, size), BF16)],
        [own_second, x_sib, exchange(d_second, bits=1)],
        flops,
        [pltpu.VMEM((block, size), F32)],
    )
    from_plane = across_chips([own, *others])[1:]
    from_neighbour = swap_replicas(send_second, bits=1)
    d_slots = call(
        functools.partial(token_kernel, features),
        [pair] * chips,
        [w_held, d_first, d_second],
        2 * slots * width * columns,
    )
    from_neighbour, d_slots = lax.optimization_barrier((from_neighbour, d_slots))
    own_second, *others_second = call(
        sum_blocks_kernel,
        [shaped((half, size), F32)] + [shaped((half, size), BF16)] * (chips - 1),
        [keep_second, from_neighbour],
        chips * half * size,
    )
    second_plane = across_chips([own_second, *others_second])[1:]
    from_plane, own_second = lax.optimization_barrier((from_plane, own_second))
    keep_first, send_first = call(
        sum_halves_kernel,
        [shaped((half, size), F32), shaped((half, size), BF16)],
        [own, *from_plane],
        chips * block * size,
        [pltpu.VMEM((block, size), F32)],
    )
    first = (keep_first + swap_replicas(send_first, bits=1).astype(F32)).astype(BF16)
    second = own_second
    for other in second_plane:
        second = second + other.astype(F32)
    second = second.astype(BF16)
    d_slots, _, _ = lax.optimization_barrier((d_slots, first, second))
    returned = across_chips(d_slots)
    bits = 2
    while 2 * bits < replicas:
        first, second = [(v.astype(F32) + swap_replicas(v, bits=bits).astype(F32)).astype(BF16) for v in (first, second)]
        bits *= 2
    if bits < replicas:
        first, second = [(v.astype(F32) + swap_replicas(v, bits=bits).astype(F32)).astype(BF16) for v in (first, second)]
    joined = [first, swap_replicas(first, bits=1), second, swap_replicas(second, bits=1)]
    near, far = call(sort_kernel, [sorted_half] * 2, returned, slots * width)
    far = exchange(far, bits=1)
    (grad_tokens,) = call(
        functools.partial(unpack_kernel, peers, capacity),
        [shaped((rows, width), BF16)],
        [users, near, far],
        2 * slots * rows * width,
        [pltpu.VMEM((slots, width), BF16), users_scratch, pltpu.SemaphoreType.DMA((1,))],
        [HBM, VMEM, VMEM],
    )
    joined[-1], grad_tokens = lax.optimization_barrier((joined[-1], grad_tokens))
    (grad_weight,) = call(
        functools.partial(join_kernel, features),
        [shaped((block, columns), F32)],
        joined,
        block * columns,
    )
    return (attended[None], grad_tokens[None], grad_weight)


def power_of_two(value):
    return value > 1 and value & (value - 1) == 0


def body(tokens, user_of_row, proj_weight, norm_gain, grad_out):
    peers = lax.axis_size("dp")
    replicas = lax.axis_size("replica")
    capacity = 2 * tokens.shape[1] // peers
    aligned = capacity % 16 == 0 and proj_weight.shape[0] // peers % 128 == 0
    run = direct_body if aligned and power_of_two(peers) and power_of_two(replicas) else general_body
    return run(tokens, user_of_row, proj_weight, norm_gain, grad_out)


def solution(mesh):
    return jax.shard_map(
        body,
        mesh=mesh,
        in_specs=(P("replica", "dp", None), P("replica", None), P(), P(), P("replica", "dp", None)),
        out_specs=(P("replica", "dp", None), P("replica", "dp", None), P("dp", None)),
        check_vma=False,
    )
```

```python
import functools

import jax
import jax.numpy as jnp
from jax import lax
from jax.experimental import pallas as pl
from jax.experimental.pallas import tpu as pltpu
from jax.sharding import PartitionSpec as P

HEADS = 4
HEAD_DIM = 128
UPO = 4


def silu_grad(preact):
    sigmoid_p = jax.nn.sigmoid(preact)
    return sigmoid_p * (1.0 + preact * (1.0 - sigmoid_p))


def attend(activated, gain, slot_user, slot_order):
    slot_total = activated.shape[0]
    split_acts = activated.astype(jnp.float32).reshape(slot_total, 3, HEADS, HEAD_DIM)
    queries = split_acts[:, 0]
    keys_h = split_acts[:, 1]
    values = split_acts[:, 2]
    scores = jnp.einsum(
        "qhd,khd->hqk", queries, keys_h, precision=lax.Precision.HIGHEST
    ) * HEAD_DIM ** (-0.5)
    visible = (
        (slot_user[:, None] == slot_user[None, :])
        & (slot_order[None, :] <= slot_order[:, None])
        & (slot_user[:, None] >= 0)
    )
    weights = jnp.where(visible[None], jax.nn.silu(scores), 0.0)
    mixed = jnp.einsum("hqk,khd->qhd", weights, values, precision=lax.Precision.HIGHEST).reshape(
        slot_total, HEADS * HEAD_DIM
    )
    mean_row = jnp.mean(mixed, axis=1, keepdims=True)
    centered = mixed - mean_row
    variance = jnp.mean(centered * centered, axis=1, keepdims=True)
    return centered * lax.rsqrt(variance + 1e-06) * gain


def block_pass(activated, gain, slot_user, slot_order, cotangent):

    def forward(acts):
        return attend(acts, gain, slot_user, slot_order)

    normed, pull = jax.vjp(forward, activated)
    (d_acts,) = pull(cotangent.astype(jnp.float32))
    return (normed.astype(jnp.bfloat16), d_acts)


def general_body(tokens, user_of_row, proj_weight, norm_gain, grad_out):
    peer_count = lax.axis_size("dp")
    self_index = lax.axis_index("dp")
    row_count = tokens.shape[1]
    width = proj_weight.shape[0]
    capacity = 2 * row_count // peer_count
    slot_count = peer_count * capacity
    routing = user_of_row[0]
    owners = (routing // UPO).reshape(peer_count, row_count)
    peer_ids = jnp.arange(peer_count, dtype=jnp.int32)
    inbound = (owners == self_index).astype(jnp.int32)
    in_rank = jnp.cumsum(inbound, axis=1) - 1
    matches = (
        (inbound[:, None, :] == 1)
        & (in_rank[:, None, :] == jnp.arange(capacity, dtype=jnp.int32)[None, :, None])
    ).astype(jnp.int32)
    users_src = routing.reshape(peer_count, row_count)
    slot_user = jnp.sum(matches * (users_src[:, None, :] + 1), axis=2).reshape(slot_count) - 1
    order_src = jnp.arange(peer_count * row_count, dtype=jnp.int32).reshape(peer_count, row_count)
    slot_order = jnp.sum(matches * order_src[:, None, :], axis=2).reshape(slot_count)
    own_owner = lax.dynamic_slice_in_dim(owners, self_index, 1, 0)[0]
    to_peer = (own_owner[:, None] == peer_ids[None, :]).astype(jnp.int32)
    out_rank = jnp.sum(jnp.cumsum(to_peer, axis=0) * to_peer, axis=1) - 1
    position = own_owner * capacity + out_rank
    rows_x = tokens[0]
    cotangent = grad_out[0]
    contract_cols = (((1,), (1,)), ((), ()))
    contract_rows = (((0,), (0,)), ((), ()))
    outgoing = jnp.zeros((slot_count, width), rows_x.dtype).at[position].set(rows_x)
    arrived = lax.all_to_all(outgoing, "dp", split_axis=0, concat_axis=0, tiled=True)
    preact = jnp.dot(arrived, proj_weight, preferred_element_type=jnp.float32)
    activated = jax.nn.silu(preact).astype(jnp.bfloat16)
    attended, d_acts = block_pass(activated, norm_gain, slot_user, slot_order, cotangent)
    d_acts = lax.optimization_barrier(d_acts)
    d_pre = (d_acts.astype(jnp.float32) * silu_grad(preact)).astype(jnp.bfloat16)
    d_slots = lax.dot_general(
        d_pre, proj_weight, contract_cols, preferred_element_type=jnp.float32
    ).astype(jnp.bfloat16)
    returned = lax.all_to_all(d_slots, "dp", split_axis=0, concat_axis=0, tiled=True)
    grad_tokens = returned[position]
    weight_shard = lax.psum_scatter(
        lax.dot_general(arrived, d_pre, contract_rows, preferred_element_type=jnp.float32),
        "dp",
        scatter_dimension=0,
        tiled=True,
    )
    grad_weight = lax.psum(weight_shard, "replica")
    return (attended[None], grad_tokens[None], grad_weight)


F32 = jnp.float32
BF16 = jnp.bfloat16
ROWS_BY_COLS = (((1,), (0,)), ((), ()))
COLS_BY_COLS = (((1,), (1,)), ((), ()))
ROWS_BY_ROWS = (((0,), (0,)), ((), ()))
VMEM_LIMIT = 32 * 1024 * 1024
HBM = pl.BlockSpec(memory_space=pltpu.HBM)
VMEM = pl.BlockSpec(memory_space=pltpu.VMEM)


def matmul(left, right, contract=ROWS_BY_COLS):
    return lax.dot_general(left, right, contract, preferred_element_type=F32)


def call(kernel, outs, operands, flops, scratch=(), specs=None):
    specs = specs or [VMEM] * len(operands)
    nbytes = sum(a.size * a.dtype.itemsize for a in operands)
    nbytes += sum(o.size * o.dtype.itemsize for o in outs)
    return pl.pallas_call(
        kernel,
        out_shape=outs,
        in_specs=specs,
        out_specs=[VMEM] * len(outs),
        scratch_shapes=list(scratch),
        compiler_params=pltpu.CompilerParams(vmem_limit_bytes=VMEM_LIMIT),
        cost_estimate=pl.CostEstimate(flops=flops, bytes_accessed=nbytes, transcendentals=0),
    )(*[pltpu.with_memory_space_constraint(a, pltpu.HBM) if s is HBM else a for a, s in zip(operands, specs)])


def shaped(shape, dtype):
    return jax.ShapeDtypeStruct(shape, dtype)


def running_count(flags):
    length = flags.shape[1]
    at = lax.broadcasted_iota(jnp.int32, (length, length), 0)
    upto = lax.broadcasted_iota(jnp.int32, (length, length), 1)
    return matmul(flags, (at <= upto).astype(F32))


def own_placement(users_ref, me, peers, capacity, paired):
    owner = lax.div(users_ref[pl.ds(me, 1), :], UPO)
    rows = owner.shape[1]
    match = (lax.broadcasted_iota(jnp.int32, (peers, rows), 0) == owner).astype(F32)
    rank = jnp.sum(running_count(match) * match, axis=0, keepdims=True) - 1.0
    block = owner ^ me
    if not paired:
        block = lax.div(block, 2) + lax.rem(block, 2) * (peers // 2)
    key = block * capacity + rank.astype(jnp.int32)
    return (lax.broadcasted_iota(jnp.int32, (peers * capacity, rows), 0) == key).astype(BF16)


def block_order(peers):
    return [*range(0, peers, 2), *range(1, peers, 2)]


def fetch(pairs, sems):
    copies = [pltpu.make_async_copy(src, dst, sems.at[i]) for i, (src, dst) in enumerate(pairs)]
    for copy in copies:
        copy.start()
    return copies


def pack_kernel(peers, capacity, users_hbm, tokens_hbm, *refs):
    *out_refs, users, rows, sems = refs
    users_copy, rows_copy = fetch([(users_hbm, users), (tokens_hbm, rows)], sems)
    me = lax.axis_index("dp")
    users_copy.wait()
    place = own_placement(users, me, peers, capacity, True)
    rows_copy.wait()
    packed = matmul(place, rows[...]).astype(BF16)
    for i, out_ref in enumerate(out_refs):
        out_ref[...] = packed[2 * i * capacity : 2 * (i + 1) * capacity]


def sort_kernel(chips, *refs):
    in_refs, mine_ref, other_refs = refs[:chips], refs[chips], refs[chips + 1 :]
    capacity = in_refs[0].shape[0] // 2
    for i, in_ref in enumerate(in_refs):
        mine_ref[i * capacity : (i + 1) * capacity, :] = in_ref[:capacity, :]
        other_refs[i][...] = in_ref[capacity:, :]


def sort_arrived_kernel(chips, *refs):
    in_refs, (mine_ref, other_ref, mine_part_ref, other_part_ref) = refs[:chips], refs[chips:]
    me = lax.axis_index("dp")
    capacity = in_refs[0].shape[0] // 2
    block = in_refs[0].shape[1] // (2 * chips)
    for i, in_ref in enumerate(in_refs):
        rows = slice(i * capacity, (i + 1) * capacity)
        mine_ref[rows, :] = in_ref[:capacity, :]
        other_ref[rows, :] = in_ref[capacity:, :]
    for i in range(chips):
        columns = slice(i * block, (i + 1) * block)
        theirs = pl.multiple_of((me ^ (2 * i + 1)) * block, block)
        ours = pl.multiple_of((me ^ (2 * i)) * block, block)
        mine_part_ref[:, columns] = mine_ref[:, pl.ds(theirs, block)]
        other_part_ref[:, columns] = other_ref[:, pl.ds(ours, block)]


def slot_codes(users_ref, me, peers, capacity):
    order = block_order(peers)
    users = jnp.concatenate([users_ref[pl.ds(me ^ m, 1), :] for m in order], axis=0)
    rows = users.shape[1]
    match = (lax.div(users, UPO) == me).astype(F32)
    rank = running_count(match) * match - 1.0
    position = lax.broadcasted_iota(jnp.int32, (1, rows), 1)
    slot = lax.broadcasted_iota(jnp.int32, (capacity, rows), 0).astype(F32)
    codes = []
    for i, m in enumerate(order):
        code = (users[i : i + 1] + 1) * (peers * rows) + (me ^ m) * rows + position
        picked = jnp.where(rank[i : i + 1] == slot, code.astype(F32), 0.0)
        codes.append(jnp.sum(picked, axis=1, keepdims=True))
    return jnp.concatenate(codes, axis=0)


def prep_kernel(peers, capacity, users_hbm, gain_ref, w_hbm, grad_hbm, w_ref, grad_ref, code_ref, key_ref, place_ref, users, grad, sems):
    users_copy, grad_copy, w_copy = fetch([(users_hbm, users), (grad_hbm, grad), (w_hbm, w_ref)], sems)
    me = lax.axis_index("dp")
    users_copy.wait()
    code = jnp.broadcast_to(slot_codes(users, me, peers, capacity), code_ref.shape)
    code_ref[...] = code
    key_ref[...] = code.T[0 : key_ref.shape[0]]
    place_ref[...] = own_placement(users, me, peers, capacity, False)
    grad_copy.wait()
    for i, m in enumerate(block_order(peers)):
        at = pl.multiple_of((me ^ m) * capacity, capacity)
        grad_ref[i * capacity : (i + 1) * capacity, :] = grad[pl.ds(at, capacity), :].astype(F32) * gain_ref[...]
    w_copy.wait()


def attend_kernel(peers, capacity, batch_rows, gain_ref, w_ref, grad, code_ref, key_ref, near_ref, far_ref, *refs):
    attended_ref, *d_refs, x_own_ref, x, act, slope = refs
    me = lax.axis_index("dp")
    slots = peers * capacity
    width, columns = w_ref.shape
    features = gain_ref.shape[1]
    block = width // peers
    x[: slots // 2, :] = near_ref[...]
    x[slots // 2 :, :] = far_ref[...]
    for i in range(peers // 2):
        at = pl.multiple_of((me ^ (2 * i)) * block, block)
        x_own_ref[:, i * block : (i + 1) * block] = x[:, pl.ds(at, block)]
    gain = gain_ref[...]
    step = 2 * HEAD_DIM
    for c in range(0, columns, step):
        preact = matmul(x[...], w_ref[:, c : c + step])
        gate = 0.5 * jnp.tanh(0.5 * preact) + 0.5
        silu = preact * gate
        act[:, c : c + step] = silu.astype(BF16)
        slope[:, c : c + step] = gate + silu * (1.0 - gate)

    code = code_ref[:, 0:1]
    code_of_key = key_ref[0:1, :]
    first = (lax.div(code.astype(jnp.int32), batch_rows) * batch_rows).astype(F32)
    first = jnp.where(code > 0.0, first, code + 1.0)
    visible = (code_of_key <= code) & (code_of_key >= first)

    def head(base, h):
        return act[:, base + h * HEAD_DIM : base + (h + 1) * HEAD_DIM]

    scale = HEAD_DIM**-0.5
    weights, slopes, mixed = [], [], []
    for h in range(HEADS):
        scores = matmul(head(0, h), head(features, h), COLS_BY_COLS) * scale
        gate = 0.5 * jnp.tanh(0.5 * scores) + 0.5
        silu = scores * gate
        weight = jnp.where(visible, silu, 0.0).astype(BF16)
        slopes.append(jnp.where(visible, (gate + silu * (1.0 - gate)) * scale, 0.0))
        weights.append(weight)
        mixed.append(matmul(weight, head(2 * features, h)))
    mean = sum(jnp.sum(v, axis=1, keepdims=True) for v in mixed) / features
    centered = [v - mean for v in mixed]
    variance = sum(jnp.sum(v * v, axis=1, keepdims=True) for v in centered) / features
    inverse = lax.rsqrt(variance + 1e-06)
    unit = [v * inverse for v in centered]

    def part(ref, h):
        return ref[:, h * HEAD_DIM : (h + 1) * HEAD_DIM]

    grads = [part(grad, h) for h in range(HEADS)]
    for h in range(HEADS):
        normed = (unit[h] * part(gain, h)).astype(BF16)
        for i, m in enumerate(block_order(peers)):
            at = pl.multiple_of((me ^ m) * capacity, capacity)
            attended_ref[pl.ds(at, capacity), h * HEAD_DIM : (h + 1) * HEAD_DIM] = normed[i * capacity : (i + 1) * capacity]
    grad_mean = sum(jnp.sum(g, axis=1, keepdims=True) for g in grads) / features
    grad_unit = sum(jnp.sum(g * u, axis=1, keepdims=True) for g, u in zip(grads, unit)) / features
    per = HEADS // len(d_refs)
    for h in range(HEADS):
        d_ref, at = d_refs[h // per], h % per * HEAD_DIM
        d_mixed = ((grads[h] - grad_mean - unit[h] * grad_unit) * inverse).astype(BF16)
        d_scores = (matmul(d_mixed, head(2 * features, h), COLS_BY_COLS) * slopes[h]).astype(BF16)
        d_query = matmul(d_scores, head(features, h))
        d_key = matmul(d_scores, head(0, h), ROWS_BY_ROWS)
        d_value = matmul(weights[h], d_mixed, ROWS_BY_ROWS)
        for j, d in enumerate((d_query, d_key, d_value)):
            to = j * per * HEAD_DIM + at
            d_ref[:, to : to + HEAD_DIM] = (d * part(slope, j * HEADS + h)).astype(BF16)


def own_weight_kernel(x_ref, near_part_ref, far_part_ref, d_first_ref, d_second_ref, first_ref, second_ref, x_sib_ref):
    half = near_part_ref.shape[0]
    x_sib_ref[:half, :] = near_part_ref[...]
    x_sib_ref[half:, :] = far_part_ref[...]
    first_ref[...] = matmul(x_ref[...], d_first_ref[...], ROWS_BY_ROWS)
    second_ref[...] = matmul(x_ref[...], d_second_ref[...], ROWS_BY_ROWS)


def weight_block(i, own_ref, x_sib_ref, d_sib_ref, block):
    at = slice(i * block, (i + 1) * block)
    return own_ref[at, :] + matmul(x_sib_ref[:, at], d_sib_ref[...], ROWS_BY_ROWS)


def weight_kernel(own_ref, x_sib_ref, d_sib_ref, *out_refs):
    block = out_refs[0].shape[0]
    for i, out_ref in enumerate(out_refs):
        out_ref[...] = weight_block(i, own_ref, x_sib_ref, d_sib_ref, block).astype(out_ref.dtype)


def halves(half):
    side = lax.rem(lax.axis_index("replica"), 2)
    return pl.multiple_of(side * half, half), pl.multiple_of((1 - side) * half, half)


def weight_halves_kernel(blocks, own_ref, x_sib_ref, d_sib_ref, keep_ref, send_ref, held):
    block = held.shape[0]
    half = block // 2
    keep_at, send_at = halves(half)
    for i in range(blocks):
        held[...] = weight_block(i, own_ref, x_sib_ref, d_sib_ref, block)
        rows = slice(i * half, (i + 1) * half)
        keep_ref[rows, :] = held[pl.ds(keep_at, half), :]
        send_ref[rows, :] = held[pl.ds(send_at, half), :].astype(BF16)


def sum_halves_kernel(own_ref, *refs):
    *in_refs, keep_ref, send_ref, held = refs
    half = held.shape[0] // 2
    total = own_ref[...]
    for in_ref in in_refs:
        total = total + in_ref[...].astype(F32)
    held[...] = total
    keep_at, send_at = halves(half)
    keep_ref[...] = held[pl.ds(keep_at, half), :]
    send_ref[...] = held[pl.ds(send_at, half), :].astype(BF16)


def sum_blocks_kernel(keep_ref, in_ref, *out_refs):
    half = out_refs[0].shape[0]
    for i, out_ref in enumerate(out_refs):
        rows = slice(i * half, (i + 1) * half)
        out_ref[...] = (keep_ref[rows, :] + in_ref[rows, :].astype(F32)).astype(out_ref.dtype)


def join_kernel(features, *refs):
    *in_refs, out_ref = refs
    half = out_ref.shape[0] // 2
    keep_at, send_at = halves(half)
    per = in_refs[0].shape[1] // 3
    for p in range(2):
        for in_ref, at in ((in_refs[2 * p], keep_at), (in_refs[2 * p + 1], send_at)):
            for j in range(3):
                to = j * features + p * per
                out_ref[pl.ds(at, half), to : to + per] = in_ref[:, j * per : (j + 1) * per].astype(F32)


def token_kernel(features, w_ref, *refs):
    d_refs, out_refs = refs[:2], refs[2:]
    capacity = out_refs[0].shape[0] // 2
    slots = d_refs[0].shape[0]
    per = d_refs[0].shape[1] // 3
    total = None
    for p, d_ref in enumerate(d_refs):
        for j in range(3):
            at = j * features + p * per
            term = matmul(d_ref[:, j * per : (j + 1) * per], w_ref[:, at : at + per], COLS_BY_COLS)
            total = term if total is None else total + term
    for i, out_ref in enumerate(out_refs):
        for j in range(2):
            at = j * (slots // 2) + i * capacity
            out_ref[j * capacity : (j + 1) * capacity, :] = total[at : at + capacity].astype(BF16)


def unpack_kernel(place_ref, near_ref, *refs):
    *far_refs, out_ref, held = refs
    at = near_ref.shape[0]
    held[:at, :] = near_ref[...]
    for far_ref in far_refs:
        held[at : at + far_ref.shape[0], :] = far_ref[...]
        at += far_ref.shape[0]
    out_ref[...] = matmul(place_ref[...], held[...], ROWS_BY_ROWS).astype(BF16)


def swap(array, axis, size, bits):
    return lax.ppermute(array, axis, [(i, i ^ bits) for i in range(size)])


def direct_body(tokens, user_of_row, proj_weight, norm_gain, grad_out):
    peers = lax.axis_size("dp")
    replicas = lax.axis_size("replica")
    rows = tokens.shape[1]
    width, columns = proj_weight.shape
    features = grad_out.shape[2]
    capacity = 2 * rows // peers
    slots = peers * capacity
    chips = peers // 2
    block = width // peers
    half = block // 2
    size = columns // 2
    users = user_of_row.reshape(peers, rows)
    gain = norm_gain.reshape(1, features)
    exchange = functools.partial(swap, axis="dp", size=peers)
    swap_replicas = functools.partial(swap, axis="replica", size=replicas)
    pair = shaped((2 * capacity, width), BF16)
    sorted_half = shaped((slots // 2, width), BF16)
    users_scratch = pltpu.VMEM((peers, rows), jnp.int32)

    def across_chips(arrays):
        return [arrays[0]] + [exchange(arrays[i], bits=2 * i) for i in range(1, chips)]

    packed = call(
        functools.partial(pack_kernel, peers, capacity),
        [pair] * chips,
        [users, tokens[0]],
        2 * slots * rows * width,
        [users_scratch, pltpu.VMEM((rows, width), BF16), pltpu.SemaphoreType.DMA((2,))],
        [HBM, HBM],
    )
    arrived = across_chips(packed)
    prepared = call(
        functools.partial(prep_kernel, peers, capacity),
        [
            shaped((width, columns), BF16),
            shaped((slots, features), F32),
            shaped((slots, HEAD_DIM), F32),
            shaped((8, slots), F32),
            shaped((slots, rows), BF16),
        ],
        [users, gain, proj_weight, grad_out[0]],
        2 * slots * slots * rows,
        [users_scratch, pltpu.VMEM((slots, features), BF16), pltpu.SemaphoreType.DMA((3,))],
        [HBM, VMEM, HBM, HBM],
    )
    arrived, (w_held, grad, code, key, place) = lax.optimization_barrier((arrived, prepared))
    near, far_sib, near_part, far_part = call(
        functools.partial(sort_arrived_kernel, chips),
        [sorted_half] * 2 + [shaped((slots // 2, width // 2), BF16)] * 2,
        arrived,
        slots * width,
    )
    far, near_part = lax.optimization_barrier((exchange(far_sib, bits=1), exchange(near_part, bits=1)))
    attended, d_first, d_second, x_own = call(
        functools.partial(attend_kernel, peers, capacity, peers * rows),
        [shaped((slots, features), BF16)] + [shaped((slots, size), BF16)] * 2 + [shaped((slots, width // 2), BF16)],
        [gain, w_held, grad, code, key, near, far],
        2 * slots * width * columns + 14 * slots * slots * features,
        [
            pltpu.VMEM((slots, width), BF16),
            pltpu.VMEM((slots, columns), BF16),
            pltpu.VMEM((slots, columns), F32),
        ],
    )
    flops = slots * width * size
    own_first, own_second, x_sib = call(
        own_weight_kernel,
        [shaped((width // 2, size), F32)] * 2 + [shaped((slots, width // 2), BF16)],
        [x_own, near_part, far_part, d_first, d_second],
        2 * flops,
    )
    own, *others = call(
        weight_kernel,
        [shaped((block, size), F32)] + [shaped((block, size), BF16)] * (chips - 1),
        [own_first, x_sib, exchange(d_first, bits=1)],
        flops,
    )
    keep_second, send_second = call(
        functools.partial(weight_halves_kernel, chips),
        [shaped((chips * half, size), F32), shaped((chips * half, size), BF16)],
        [own_second, x_sib, exchange(d_second, bits=1)],
        flops,
        [pltpu.VMEM((block, size), F32)],
    )
    from_plane = across_chips([own, *others])[1:]
    from_neighbour = swap_replicas(send_second, bits=1)
    d_slots = call(
        functools.partial(token_kernel, features),
        [pair] * chips,
        [w_held, d_first, d_second],
        2 * slots * width * columns,
    )
    from_neighbour, d_slots = lax.optimization_barrier((from_neighbour, d_slots))
    own_second, *others_second = call(
        sum_blocks_kernel,
        [shaped((half, size), F32)] + [shaped((half, size), BF16)] * (chips - 1),
        [keep_second, from_neighbour],
        chips * half * size,
    )
    second_plane = across_chips([own_second, *others_second])[1:]
    from_plane, own_second = lax.optimization_barrier((from_plane, own_second))
    keep_first, send_first = call(
        sum_halves_kernel,
        [shaped((half, size), F32), shaped((half, size), BF16)],
        [own, *from_plane],
        chips * block * size,
        [pltpu.VMEM((block, size), F32)],
    )
    first = (keep_first + swap_replicas(send_first, bits=1).astype(F32)).astype(BF16)
    second = own_second
    for other in second_plane:
        second = second + other.astype(F32)
    second = second.astype(BF16)
    d_slots, _ = lax.optimization_barrier((d_slots, keep_first))
    returned = across_chips(d_slots)
    bits = 2
    while 2 * bits < replicas:
        first, second = [(v.astype(F32) + swap_replicas(v, bits=bits).astype(F32)).astype(BF16) for v in (first, second)]
        bits *= 2
    if bits < replicas:
        first, second = [(v.astype(F32) + swap_replicas(v, bits=bits).astype(F32)).astype(BF16) for v in (first, second)]
    joined = [first, swap_replicas(first, bits=1), second, swap_replicas(second, bits=1)]
    near, *far = call(
        functools.partial(sort_kernel, chips),
        [sorted_half] + [shaped((capacity, width), BF16)] * chips,
        returned,
        slots * width,
    )
    far = [exchange(a, bits=1) for a in far]
    (grad_tokens,) = call(
        unpack_kernel,
        [shaped((rows, width), BF16)],
        [place, near, *far],
        2 * slots * rows * width,
        [pltpu.VMEM((slots, width), BF16)],
    )
    joined[-1], grad_tokens = lax.optimization_barrier((joined[-1], grad_tokens))
    (grad_weight,) = call(
        functools.partial(join_kernel, features),
        [shaped((block, columns), F32)],
        joined,
        block * columns,
    )
    return (attended[None], grad_tokens[None], grad_weight)


def power_of_two(value):
    return value > 1 and value & (value - 1) == 0


def body(tokens, user_of_row, proj_weight, norm_gain, grad_out):
    peers = lax.axis_size("dp")
    replicas = lax.axis_size("replica")
    capacity = 2 * tokens.shape[1] // peers
    aligned = capacity % 16 == 0 and proj_weight.shape[0] // peers % 128 == 0
    run = direct_body if aligned and power_of_two(peers) and power_of_two(replicas) else general_body
    return run(tokens, user_of_row, proj_weight, norm_gain, grad_out)


def solution(mesh):
    return jax.shard_map(
        body,
        mesh=mesh,
        in_specs=(P("replica", "dp", None), P("replica", None), P(), P(), P("replica", "dp", None)),
        out_specs=(P("replica", "dp", None), P("replica", "dp", None), P("dp", None)),
        check_vma=False,
    )
```

```python
import functools

import jax
import jax.numpy as jnp
from jax import lax
from jax.experimental import pallas as pl
from jax.experimental.pallas import tpu as pltpu
from jax.sharding import PartitionSpec as P

HEADS = 4
HEAD_DIM = 128
UPO = 4


def silu_grad(preact):
    sigmoid_p = jax.nn.sigmoid(preact)
    return sigmoid_p * (1.0 + preact * (1.0 - sigmoid_p))


def attend(activated, gain, slot_user, slot_order):
    slot_total = activated.shape[0]
    split_acts = activated.astype(jnp.float32).reshape(slot_total, 3, HEADS, HEAD_DIM)
    queries = split_acts[:, 0]
    keys_h = split_acts[:, 1]
    values = split_acts[:, 2]
    scores = jnp.einsum(
        "qhd,khd->hqk", queries, keys_h, precision=lax.Precision.HIGHEST
    ) * HEAD_DIM ** (-0.5)
    visible = (
        (slot_user[:, None] == slot_user[None, :])
        & (slot_order[None, :] <= slot_order[:, None])
        & (slot_user[:, None] >= 0)
    )
    weights = jnp.where(visible[None], jax.nn.silu(scores), 0.0)
    mixed = jnp.einsum("hqk,khd->qhd", weights, values, precision=lax.Precision.HIGHEST).reshape(
        slot_total, HEADS * HEAD_DIM
    )
    mean_row = jnp.mean(mixed, axis=1, keepdims=True)
    centered = mixed - mean_row
    variance = jnp.mean(centered * centered, axis=1, keepdims=True)
    return centered * lax.rsqrt(variance + 1e-06) * gain


def block_pass(activated, gain, slot_user, slot_order, cotangent):

    def forward(acts):
        return attend(acts, gain, slot_user, slot_order)

    normed, pull = jax.vjp(forward, activated)
    (d_acts,) = pull(cotangent.astype(jnp.float32))
    return (normed.astype(jnp.bfloat16), d_acts)


def general_body(tokens, user_of_row, proj_weight, norm_gain, grad_out):
    peer_count = lax.axis_size("dp")
    self_index = lax.axis_index("dp")
    row_count = tokens.shape[1]
    width = proj_weight.shape[0]
    capacity = 2 * row_count // peer_count
    slot_count = peer_count * capacity
    routing = user_of_row[0]
    owners = (routing // UPO).reshape(peer_count, row_count)
    peer_ids = jnp.arange(peer_count, dtype=jnp.int32)
    inbound = (owners == self_index).astype(jnp.int32)
    in_rank = jnp.cumsum(inbound, axis=1) - 1
    matches = (
        (inbound[:, None, :] == 1)
        & (in_rank[:, None, :] == jnp.arange(capacity, dtype=jnp.int32)[None, :, None])
    ).astype(jnp.int32)
    users_src = routing.reshape(peer_count, row_count)
    slot_user = jnp.sum(matches * (users_src[:, None, :] + 1), axis=2).reshape(slot_count) - 1
    order_src = jnp.arange(peer_count * row_count, dtype=jnp.int32).reshape(peer_count, row_count)
    slot_order = jnp.sum(matches * order_src[:, None, :], axis=2).reshape(slot_count)
    own_owner = lax.dynamic_slice_in_dim(owners, self_index, 1, 0)[0]
    to_peer = (own_owner[:, None] == peer_ids[None, :]).astype(jnp.int32)
    out_rank = jnp.sum(jnp.cumsum(to_peer, axis=0) * to_peer, axis=1) - 1
    position = own_owner * capacity + out_rank
    rows_x = tokens[0]
    cotangent = grad_out[0]
    contract_cols = (((1,), (1,)), ((), ()))
    contract_rows = (((0,), (0,)), ((), ()))
    outgoing = jnp.zeros((slot_count, width), rows_x.dtype).at[position].set(rows_x)
    arrived = lax.all_to_all(outgoing, "dp", split_axis=0, concat_axis=0, tiled=True)
    preact = jnp.dot(arrived, proj_weight, preferred_element_type=jnp.float32)
    activated = jax.nn.silu(preact).astype(jnp.bfloat16)
    attended, d_acts = block_pass(activated, norm_gain, slot_user, slot_order, cotangent)
    d_acts = lax.optimization_barrier(d_acts)
    d_pre = (d_acts.astype(jnp.float32) * silu_grad(preact)).astype(jnp.bfloat16)
    d_slots = lax.dot_general(
        d_pre, proj_weight, contract_cols, preferred_element_type=jnp.float32
    ).astype(jnp.bfloat16)
    returned = lax.all_to_all(d_slots, "dp", split_axis=0, concat_axis=0, tiled=True)
    grad_tokens = returned[position]
    weight_shard = lax.psum_scatter(
        lax.dot_general(arrived, d_pre, contract_rows, preferred_element_type=jnp.float32),
        "dp",
        scatter_dimension=0,
        tiled=True,
    )
    grad_weight = lax.psum(weight_shard, "replica")
    return (attended[None], grad_tokens[None], grad_weight)


F32 = jnp.float32
BF16 = jnp.bfloat16
ROWS_BY_COLS = (((1,), (0,)), ((), ()))
COLS_BY_COLS = (((1,), (1,)), ((), ()))
ROWS_BY_ROWS = (((0,), (0,)), ((), ()))
VMEM_LIMIT = 32 * 1024 * 1024
HBM = pl.BlockSpec(memory_space=pltpu.HBM)
VMEM = pl.BlockSpec(memory_space=pltpu.VMEM)


def matmul(left, right, contract=ROWS_BY_COLS):
    return lax.dot_general(left, right, contract, preferred_element_type=F32)


def call(kernel, outs, operands, flops, scratch=(), specs=None):
    specs = specs or [VMEM] * len(operands)
    nbytes = sum(a.size * a.dtype.itemsize for a in operands)
    nbytes += sum(o.size * o.dtype.itemsize for o in outs)
    return pl.pallas_call(
        kernel,
        out_shape=outs,
        in_specs=specs,
        out_specs=[VMEM] * len(outs),
        scratch_shapes=list(scratch),
        compiler_params=pltpu.CompilerParams(vmem_limit_bytes=VMEM_LIMIT),
        cost_estimate=pl.CostEstimate(flops=flops, bytes_accessed=nbytes, transcendentals=0),
    )(*[pltpu.with_memory_space_constraint(a, pltpu.HBM) if s is HBM else a for a, s in zip(operands, specs)])


def shaped(shape, dtype):
    return jax.ShapeDtypeStruct(shape, dtype)


def running_count(flags):
    length = flags.shape[1]
    at = lax.broadcasted_iota(jnp.int32, (length, length), 0)
    upto = lax.broadcasted_iota(jnp.int32, (length, length), 1)
    return matmul(flags, (at <= upto).astype(F32))


def own_placement(users_ref, me, peers, capacity, paired):
    owner = lax.div(users_ref[pl.ds(me, 1), :], UPO)
    rows = owner.shape[1]
    match = (lax.broadcasted_iota(jnp.int32, (peers, rows), 0) == owner).astype(F32)
    rank = jnp.sum(running_count(match) * match, axis=0, keepdims=True) - 1.0
    block = owner ^ me
    if not paired:
        block = lax.div(block, 2) + lax.rem(block, 2) * (peers // 2)
    key = block * capacity + rank.astype(jnp.int32)
    return (lax.broadcasted_iota(jnp.int32, (peers * capacity, rows), 0) == key).astype(BF16)


def block_order(peers):
    return [*range(0, peers, 2), *range(1, peers, 2)]


def fetch(pairs, sems):
    copies = [pltpu.make_async_copy(src, dst, sems.at[i]) for i, (src, dst) in enumerate(pairs)]
    for copy in copies:
        copy.start()
    return copies


def pack_kernel(peers, capacity, users_hbm, tokens_hbm, *refs):
    *out_refs, users, rows, sems = refs
    users_copy, rows_copy = fetch([(users_hbm, users), (tokens_hbm, rows)], sems)
    me = lax.axis_index("dp")
    users_copy.wait()
    place = own_placement(users, me, peers, capacity, True)
    rows_copy.wait()
    packed = matmul(place, rows[...]).astype(BF16)
    for i, out_ref in enumerate(out_refs):
        out_ref[...] = packed[2 * i * capacity : 2 * (i + 1) * capacity]


def sort_kernel(chips, *refs):
    in_refs, mine_ref, other_refs = refs[:chips], refs[chips], refs[chips + 1 :]
    capacity = in_refs[0].shape[0] // 2
    for i, in_ref in enumerate(in_refs):
        mine_ref[i * capacity : (i + 1) * capacity, :] = in_ref[:capacity, :]
        other_refs[i][...] = in_ref[capacity:, :]


def sort_arrived_kernel(chips, *refs):
    in_refs, (mine_ref, other_ref, mine_part_ref, other_part_ref) = refs[:chips], refs[chips:]
    me = lax.axis_index("dp")
    capacity = in_refs[0].shape[0] // 2
    block = in_refs[0].shape[1] // (2 * chips)
    for i, in_ref in enumerate(in_refs):
        rows = slice(i * capacity, (i + 1) * capacity)
        mine_ref[rows, :] = in_ref[:capacity, :]
        other_ref[rows, :] = in_ref[capacity:, :]
    for i in range(chips):
        columns = slice(i * block, (i + 1) * block)
        theirs = pl.multiple_of((me ^ (2 * i + 1)) * block, block)
        ours = pl.multiple_of((me ^ (2 * i)) * block, block)
        mine_part_ref[:, columns] = mine_ref[:, pl.ds(theirs, block)]
        other_part_ref[:, columns] = other_ref[:, pl.ds(ours, block)]


def slot_codes(users_ref, me, peers, capacity):
    order = block_order(peers)
    users = jnp.concatenate([users_ref[pl.ds(me ^ m, 1), :] for m in order], axis=0)
    rows = users.shape[1]
    match = (lax.div(users, UPO) == me).astype(F32)
    rank = running_count(match) * match - 1.0
    position = lax.broadcasted_iota(jnp.int32, (1, rows), 1)
    slot = lax.broadcasted_iota(jnp.int32, (capacity, rows), 0).astype(F32)
    codes = []
    for i, m in enumerate(order):
        code = (users[i : i + 1] + 1) * (peers * rows) + (me ^ m) * rows + position
        picked = jnp.where(rank[i : i + 1] == slot, code.astype(F32), 0.0)
        codes.append(jnp.sum(picked, axis=1, keepdims=True))
    return jnp.concatenate(codes, axis=0)


def prep_kernel(peers, capacity, users_hbm, gain_ref, w_hbm, grad_hbm, w_ref, grad_ref, code_ref, key_ref, place_ref, users, grad, sems):
    users_copy, grad_copy, w_copy = fetch([(users_hbm, users), (grad_hbm, grad), (w_hbm, w_ref)], sems)
    me = lax.axis_index("dp")
    users_copy.wait()
    code = jnp.broadcast_to(slot_codes(users, me, peers, capacity), code_ref.shape)
    code_ref[...] = code
    key_ref[...] = code.T[0 : key_ref.shape[0]]
    place_ref[...] = own_placement(users, me, peers, capacity, False)
    grad_copy.wait()
    for i, m in enumerate(block_order(peers)):
        at = pl.multiple_of((me ^ m) * capacity, capacity)
        grad_ref[i * capacity : (i + 1) * capacity, :] = grad[pl.ds(at, capacity), :].astype(F32) * gain_ref[...]
    w_copy.wait()


def attend_kernel(peers, capacity, batch_rows, gain_ref, w_ref, grad, code_ref, key_ref, near_ref, far_ref, *refs):
    attended_ref, *d_refs, x_own_ref, x, act, slope = refs
    me = lax.axis_index("dp")
    slots = peers * capacity
    width, columns = w_ref.shape
    features = gain_ref.shape[1]
    block = width // peers
    x[: slots // 2, :] = near_ref[...]
    x[slots // 2 :, :] = far_ref[...]
    for i in range(peers // 2):
        at = pl.multiple_of((me ^ (2 * i)) * block, block)
        x_own_ref[:, i * block : (i + 1) * block] = x[:, pl.ds(at, block)]
    gain = gain_ref[...]
    step = 2 * HEAD_DIM
    for c in range(0, columns, step):
        preact = matmul(x[...], w_ref[:, c : c + step])
        gate = 0.5 * jnp.tanh(0.5 * preact) + 0.5
        silu = preact * gate
        act[:, c : c + step] = silu.astype(BF16)
        slope[:, c : c + step] = gate + silu * (1.0 - gate)

    code = code_ref[:, 0:1]
    code_of_key = key_ref[0:1, :]
    first = (lax.div(code.astype(jnp.int32), batch_rows) * batch_rows).astype(F32)
    first = jnp.where(code > 0.0, first, code + 1.0)
    visible = (code_of_key <= code) & (code_of_key >= first)

    def head(base, h):
        return act[:, base + h * HEAD_DIM : base + (h + 1) * HEAD_DIM]

    scale = HEAD_DIM**-0.5
    weights, slopes, mixed = [], [], []
    for h in range(HEADS):
        scores = matmul(head(0, h), head(features, h), COLS_BY_COLS) * scale
        gate = 0.5 * jnp.tanh(0.5 * scores) + 0.5
        silu = scores * gate
        weight = jnp.where(visible, silu, 0.0).astype(BF16)
        slopes.append(jnp.where(visible, (gate + silu * (1.0 - gate)) * scale, 0.0))
        weights.append(weight)
        mixed.append(matmul(weight, head(2 * features, h)))
    mean = sum(jnp.sum(v, axis=1, keepdims=True) for v in mixed) / features
    centered = [v - mean for v in mixed]
    variance = sum(jnp.sum(v * v, axis=1, keepdims=True) for v in centered) / features
    inverse = lax.rsqrt(variance + 1e-06)
    unit = [v * inverse for v in centered]

    def part(ref, h):
        return ref[:, h * HEAD_DIM : (h + 1) * HEAD_DIM]

    grads = [part(grad, h) for h in range(HEADS)]
    for h in range(HEADS):
        normed = (unit[h] * part(gain, h)).astype(BF16)
        for i, m in enumerate(block_order(peers)):
            at = pl.multiple_of((me ^ m) * capacity, capacity)
            attended_ref[pl.ds(at, capacity), h * HEAD_DIM : (h + 1) * HEAD_DIM] = normed[i * capacity : (i + 1) * capacity]
    grad_mean = sum(jnp.sum(g, axis=1, keepdims=True) for g in grads) / features
    grad_unit = sum(jnp.sum(g * u, axis=1, keepdims=True) for g, u in zip(grads, unit)) / features
    per = HEADS // len(d_refs)
    for h in range(HEADS):
        d_ref, at = d_refs[h // per], h % per * HEAD_DIM
        d_mixed = ((grads[h] - grad_mean - unit[h] * grad_unit) * inverse).astype(BF16)
        d_scores = (matmul(d_mixed, head(2 * features, h), COLS_BY_COLS) * slopes[h]).astype(BF16)
        d_query = matmul(d_scores, head(features, h))
        d_key = matmul(d_scores, head(0, h), ROWS_BY_ROWS)
        d_value = matmul(weights[h], d_mixed, ROWS_BY_ROWS)
        for j, d in enumerate((d_query, d_key, d_value)):
            to = j * per * HEAD_DIM + at
            d_ref[:, to : to + HEAD_DIM] = (d * part(slope, j * HEADS + h)).astype(BF16)


def own_weight_kernel(x_ref, near_part_ref, far_part_ref, d_first_ref, d_second_ref, first_ref, second_ref, x_sib_ref):
    half = near_part_ref.shape[0]
    x_sib_ref[:half, :] = near_part_ref[...]
    x_sib_ref[half:, :] = far_part_ref[...]
    first_ref[...] = matmul(x_ref[...], d_first_ref[...], ROWS_BY_ROWS)
    second_ref[...] = matmul(x_ref[...], d_second_ref[...], ROWS_BY_ROWS)


def weight_block(i, own_ref, x_sib_ref, d_sib_ref, block):
    at = slice(i * block, (i + 1) * block)
    return own_ref[at, :] + matmul(x_sib_ref[:, at], d_sib_ref[...], ROWS_BY_ROWS)


def weight_kernel(own_ref, x_sib_ref, d_sib_ref, *out_refs):
    block = out_refs[0].shape[0]
    for i, out_ref in enumerate(out_refs):
        out_ref[...] = weight_block(i, own_ref, x_sib_ref, d_sib_ref, block).astype(out_ref.dtype)


def halves(half):
    side = lax.rem(lax.axis_index("replica"), 2)
    return pl.multiple_of(side * half, half), pl.multiple_of((1 - side) * half, half)


def weight_halves_kernel(blocks, own_ref, x_sib_ref, d_sib_ref, keep_ref, send_ref, held):
    block = held.shape[0]
    half = block // 2
    keep_at, send_at = halves(half)
    for i in range(blocks):
        held[...] = weight_block(i, own_ref, x_sib_ref, d_sib_ref, block)
        rows = slice(i * half, (i + 1) * half)
        keep_ref[rows, :] = held[pl.ds(keep_at, half), :]
        send_ref[rows, :] = held[pl.ds(send_at, half), :].astype(BF16)


def sum_halves_kernel(own_ref, *refs):
    *in_refs, keep_ref, send_ref, held = refs
    half = held.shape[0] // 2
    total = own_ref[...]
    for in_ref in in_refs:
        total = total + in_ref[...].astype(F32)
    held[...] = total
    keep_at, send_at = halves(half)
    keep_ref[...] = held[pl.ds(keep_at, half), :]
    send_ref[...] = held[pl.ds(send_at, half), :].astype(BF16)


def sum_blocks_kernel(keep_ref, in_ref, *out_refs):
    half = out_refs[0].shape[0]
    for i, out_ref in enumerate(out_refs):
        rows = slice(i * half, (i + 1) * half)
        out_ref[...] = (keep_ref[rows, :] + in_ref[rows, :].astype(F32)).astype(out_ref.dtype)


def join_kernel(features, *refs):
    *in_refs, out_ref = refs
    half = out_ref.shape[0] // 2
    keep_at, send_at = halves(half)
    per = in_refs[0].shape[1] // 3
    for p in range(2):
        for in_ref, at in ((in_refs[2 * p], keep_at), (in_refs[2 * p + 1], send_at)):
            for j in range(3):
                to = j * features + p * per
                out_ref[pl.ds(at, half), to : to + per] = in_ref[:, j * per : (j + 1) * per].astype(F32)


def token_kernel(features, w_ref, *refs):
    d_refs, out_refs = refs[:2], refs[2:]
    capacity = out_refs[0].shape[0] // 2
    slots = d_refs[0].shape[0]
    per = d_refs[0].shape[1] // 3
    total = None
    for p, d_ref in enumerate(d_refs):
        for j in range(3):
            at = j * features + p * per
            term = matmul(d_ref[:, j * per : (j + 1) * per], w_ref[:, at : at + per], COLS_BY_COLS)
            total = term if total is None else total + term
    for i, out_ref in enumerate(out_refs):
        for j in range(2):
            at = j * (slots // 2) + i * capacity
            out_ref[j * capacity : (j + 1) * capacity, :] = total[at : at + capacity].astype(BF16)


def unpack_kernel(place_ref, near_ref, *refs):
    *far_refs, out_ref, held = refs
    at = near_ref.shape[0]
    held[:at, :] = near_ref[...]
    for far_ref in far_refs:
        held[at : at + far_ref.shape[0], :] = far_ref[...]
        at += far_ref.shape[0]
    out_ref[...] = matmul(place_ref[...], held[...], ROWS_BY_ROWS).astype(BF16)


def swap(array, axis, size, bits):
    return lax.ppermute(array, axis, [(i, i ^ bits) for i in range(size)])


def direct_body(tokens, user_of_row, proj_weight, norm_gain, grad_out):
    peers = lax.axis_size("dp")
    replicas = lax.axis_size("replica")
    rows = tokens.shape[1]
    width, columns = proj_weight.shape
    features = grad_out.shape[2]
    capacity = 2 * rows // peers
    slots = peers * capacity
    chips = peers // 2
    block = width // peers
    half = block // 2
    size = columns // 2
    users = user_of_row.reshape(peers, rows)
    gain = norm_gain.reshape(1, features)
    exchange = functools.partial(swap, axis="dp", size=peers)
    swap_replicas = functools.partial(swap, axis="replica", size=replicas)
    pair = shaped((2 * capacity, width), BF16)
    sorted_half = shaped((slots // 2, width), BF16)
    users_scratch = pltpu.VMEM((peers, rows), jnp.int32)

    def across_chips(arrays):
        return [arrays[0]] + [exchange(arrays[i], bits=2 * i) for i in range(1, chips)]

    packed = call(
        functools.partial(pack_kernel, peers, capacity),
        [pair] * chips,
        [users, tokens[0]],
        2 * slots * rows * width,
        [users_scratch, pltpu.VMEM((rows, width), BF16), pltpu.SemaphoreType.DMA((2,))],
        [HBM, HBM],
    )
    arrived = across_chips(packed)
    prepared = call(
        functools.partial(prep_kernel, peers, capacity),
        [
            shaped((width, columns), BF16),
            shaped((slots, features), F32),
            shaped((slots, HEAD_DIM), F32),
            shaped((8, slots), F32),
            shaped((slots, rows), BF16),
        ],
        [users, gain, proj_weight, grad_out[0]],
        2 * slots * slots * rows,
        [users_scratch, pltpu.VMEM((slots, features), BF16), pltpu.SemaphoreType.DMA((3,))],
        [HBM, VMEM, HBM, HBM],
    )
    arrived, (w_held, grad, code, key, place) = lax.optimization_barrier((arrived, prepared))
    near, far_sib, near_part, far_part = call(
        functools.partial(sort_arrived_kernel, chips),
        [sorted_half] * 2 + [shaped((slots // 2, width // 2), BF16)] * 2,
        arrived,
        slots * width,
    )
    far, near_part = lax.optimization_barrier((exchange(far_sib, bits=1), exchange(near_part, bits=1)))
    attended, d_first, d_second, x_own = call(
        functools.partial(attend_kernel, peers, capacity, peers * rows),
        [shaped((slots, features), BF16)] + [shaped((slots, size), BF16)] * 2 + [shaped((slots, width // 2), BF16)],
        [gain, w_held, grad, code, key, near, far],
        2 * slots * width * columns + 14 * slots * slots * features,
        [
            pltpu.VMEM((slots, width), BF16),
            pltpu.VMEM((slots, columns), BF16),
            pltpu.VMEM((slots, columns), F32),
        ],
    )
    flops = slots * width * size
    own_first, own_second, x_sib = call(
        own_weight_kernel,
        [shaped((width // 2, size), F32)] * 2 + [shaped((slots, width // 2), BF16)],
        [x_own, near_part, far_part, d_first, d_second],
        2 * flops,
    )
    own, *others = call(
        weight_kernel,
        [shaped((block, size), F32)] + [shaped((block, size), BF16)] * (chips - 1),
        [own_first, x_sib, exchange(d_first, bits=1)],
        flops,
    )
    keep_second, send_second = call(
        functools.partial(weight_halves_kernel, chips),
        [shaped((chips * half, size), F32), shaped((chips * half, size), BF16)],
        [own_second, x_sib, exchange(d_second, bits=1)],
        flops,
        [pltpu.VMEM((block, size), F32)],
    )
    from_plane = across_chips([own, *others])[1:]
    from_neighbour = swap_replicas(send_second, bits=1)
    d_slots = call(
        functools.partial(token_kernel, features),
        [pair] * chips,
        [w_held, d_first, d_second],
        2 * slots * width * columns,
    )
    from_neighbour, d_slots = lax.optimization_barrier((from_neighbour, d_slots))
    own_second, *others_second = call(
        sum_blocks_kernel,
        [shaped((half, size), F32)] + [shaped((half, size), BF16)] * (chips - 1),
        [keep_second, from_neighbour],
        chips * half * size,
    )
    second_plane = across_chips([own_second, *others_second])[1:]
    from_plane, own_second = lax.optimization_barrier((from_plane, own_second))
    keep_first, send_first = call(
        sum_halves_kernel,
        [shaped((half, size), F32), shaped((half, size), BF16)],
        [own, *from_plane],
        chips * block * size,
        [pltpu.VMEM((block, size), F32)],
    )
    first = (keep_first + swap_replicas(send_first, bits=1).astype(F32)).astype(BF16)
    second = own_second
    for other in second_plane:
        second = second + other.astype(F32)
    second = second.astype(BF16)
    d_slots, _ = lax.optimization_barrier((d_slots, keep_first))
    returned = across_chips(d_slots)
    bits = 2
    while 2 * bits < replicas:
        first, second = [(v.astype(F32) + swap_replicas(v, bits=bits).astype(F32)).astype(BF16) for v in (first, second)]
        bits *= 2
    if bits < replicas:
        first, second = [(v.astype(F32) + swap_replicas(v, bits=bits).astype(F32)).astype(BF16) for v in (first, second)]
    joined = [first, swap_replicas(first, bits=1), second, swap_replicas(second, bits=1)]
    near, far, _, _ = call(
        functools.partial(sort_arrived_kernel, chips),
        [sorted_half] * 2 + [shaped((slots // 2, width // 2), BF16)] * 2,
        returned,
        slots * width,
    )
    far = [exchange(far, bits=1)]
    (grad_tokens,) = call(
        unpack_kernel,
        [shaped((rows, width), BF16)],
        [place, near, *far],
        2 * slots * rows * width,
        [pltpu.VMEM((slots, width), BF16)],
    )
    joined[-1], grad_tokens = lax.optimization_barrier((joined[-1], grad_tokens))
    (grad_weight,) = call(
        functools.partial(join_kernel, features),
        [shaped((block, columns), F32)],
        joined,
        block * columns,
    )
    return (attended[None], grad_tokens[None], grad_weight)


def power_of_two(value):
    return value > 1 and value & (value - 1) == 0


def body(tokens, user_of_row, proj_weight, norm_gain, grad_out):
    peers = lax.axis_size("dp")
    replicas = lax.axis_size("replica")
    capacity = 2 * tokens.shape[1] // peers
    aligned = capacity % 16 == 0 and proj_weight.shape[0] // peers % 128 == 0
    run = direct_body if aligned and power_of_two(peers) and power_of_two(replicas) else general_body
    return run(tokens, user_of_row, proj_weight, norm_gain, grad_out)


def solution(mesh):
    return jax.shard_map(
        body,
        mesh=mesh,
        in_specs=(P("replica", "dp", None), P("replica", None), P(), P(), P("replica", "dp", None)),
        out_specs=(P("replica", "dp", None), P("replica", "dp", None), P("dp", None)),
        check_vma=False,
    )
```
